32 devices in a mesh: group: 2 (over x), blk: 16 (over z, y, core).
Axes of the slice: x: 2, y: 2, z: 4, core: 2. Of those that a mesh axis runs over, the one named last changes fastest.
Arguments:
- stack_wet_layers: int32 [128, 32, 128], P(('group', 'blk')), parts along dimension 0, may hold values from 0 to 20, as said below
- patch_owner: int32 [128], P('group'), parts along dimension 0, may hold values from 0 to 15, as said below
- piece_owner: int32 [512], P('group'), parts along dimension 0, may hold values from -1 to 15, as said below
- piece_neighbours: int32 [512, 8], P('group'), parts along dimension 0, may hold values from 0 to 256, as said below
- east_velocity: float32 [128, 20, 32, 128], P(('group', 'blk')), parts along dimension 0, may hold values from -6 to 6
- north_velocity: float32 [128, 20, 32, 128], P(('group', 'blk')), parts along dimension 0, may hold values from -6 to 6
- heat_anomaly: float32 [128, 20, 32, 128], P(('group', 'blk')), parts along dimension 0, may hold values from -6 to 6
- saltiness_anomaly: float32 [128, 20, 32, 128], P(('group', 'blk')), parts along dimension 0, may hold values from -6 to 6
- diffusivity_below: float32 [128, 20, 32, 128], P(('group', 'blk')), parts along dimension 0, may hold values from 0.05 to 20
Outputs:
- east_velocity_next: float32 [128, 20, 32, 128], P(('group', 'blk')), parts along dimension 0
- north_velocity_next: float32 [128, 20, 32, 128], P(('group', 'blk')), parts along dimension 0
- heat_anomaly_mixed: float32 [128, 20, 32, 128], P(('group', 'blk')), parts along dimension 0
- saltiness_mixed: float32 [128, 20, 32, 128], P(('group', 'blk')), parts along dimension 0
- sea_height_patches: float32 [448, 8, 128], P(('group', 'blk')), parts along dimension 0
The draws below stay inside these ranges and needn't reach their ends.
There are 2 independent parts, one for each index of `group`. The reference program is written for one: setup_inputs(seed, part) draws one part's arguments, and reference() takes and returns one part's arrays. A program takes and returns all parts, laid end to end along the dimension named above; each array names one. Nothing has to cross between parts.
Inputs may be any that keep to these rules, and one draw needn't show every extreme that they name: `stack_wet_layers`: ocean levels of each column; 0 on land; every column of a tile whose piece_owner is -1 is land. `patch_owner`: each device of blk owns exactly 4 blocks, a run of consecutive block numbers. `piece_owner`: -1 marks a tile left out of the solve; every device owns exactly 14 tiles; of the tiles of the blocks of one device at most 2 have the same owner, exactly 2 for some pair of devices. `piece_neighbours`: row t lists the tiles above, below, left of, right of, above-left, above-right, below-left and below-right of tile t, 256 where there is none or where that tile's owner is -1.
All inputs are finite; a program needn't handle non-finite values.
Results may differ from the reference program's by a relative error of at most 0.0003.
Values sent between devices are 32-bit elements; how exact they have to be, the bound alone decides.
A program may use at most 64 MiB of HBM per device.

```python
import math
import jax
import jax.numpy as jnp
from jax import lax

LAYER_NUMBER = 20
PATCH_CELL_HIGH = 32
PATCH_CELL_WIDE = 128
BLK_DEV = 4
SPLIT = 4
BT_DEV = 14
ITERS = 6
SUB = 4
TY = 8
TX = 128
TILES_DEV = 16
PATCH_AMOUNT = 64
NT = 256
NBX = 4
NBY = 16
CAP = 2
N_BLK = 16


def ocean_layout(key):
    keys = jax.random.split(key, 3)
    runs = jax.random.permutation(keys[0], N_BLK).astype(jnp.int32)
    block_ids = jnp.arange(PATCH_AMOUNT, dtype=jnp.int32)
    patch_owner = runs[block_ids // BLK_DEV]
    land_count = N_BLK * (TILES_DEV - BT_DEV)
    picked = jax.random.permutation(keys[1], NT - TILES_DEV).astype(jnp.int32)[:land_count] + TILES_DEV
    land = jnp.zeros((NT,), jnp.int32).at[picked].set(1)
    live = 1 - land
    ocean_rank = jnp.cumsum(live) - 1
    offset = jax.random.randint(keys[2], (), 0, N_BLK)
    piece_owner = jnp.where(live == 1, (ocean_rank // CAP + offset) % N_BLK, -1).astype(jnp.int32)
    return (runs, patch_owner, live, piece_owner)


def tile_grid(tile):
    block = tile // SUB
    inner = tile % SUB
    block_row = block // NBX
    within = block % NBX
    block_col = jnp.where(block_row % 2 == 0, within, NBX - 1 - within)
    return (block_row * SPLIT + inner, block_col)


def tile_at(grid_row, grid_col):
    block_row = grid_row // SPLIT
    block = block_row * NBX + jnp.where(block_row % 2 == 0, grid_col, NBX - 1 - grid_col)
    return block * SUB + grid_row % SPLIT


def draw_patch_owner(key, part):
    runs, patch_owner, live, piece_owner = ocean_layout(key)
    return patch_owner


def draw_piece_owner(key, part):
    runs, patch_owner, live, piece_owner = ocean_layout(key)
    return piece_owner


def draw_piece_neighbours(key, part):
    runs, patch_owner, live, piece_owner = ocean_layout(key)
    tiles = jnp.arange(NT, dtype=jnp.int32)
    grid_row, grid_col = tile_grid(tiles)
    height_cells = NBY * SPLIT
    width_cells = NBX
    columns = []
    for down, across in ((-1, 0), (1, 0), (0, -1), (0, 1), (-1, -1), (-1, 1), (1, -1), (1, 1)):
        other_row = grid_row + down
        other_col = grid_col + across
        inside = (other_row >= 0) & (other_row < height_cells) & (other_col >= 0) & (other_col < width_cells)
        target = tile_at(jnp.clip(other_row, 0, height_cells - 1), jnp.clip(other_col, 0, width_cells - 1))
        usable = inside & (live[target] == 1)
        columns.append(jnp.where(usable, target, NT))
    return jnp.stack(columns, axis=1).astype(jnp.int32)


def draw_stack_wet_layers(key, part):
    runs, patch_owner, live, piece_owner = ocean_layout(key)
    key = jax.random.fold_in(key, 7)
    keys = jax.random.split(key, 2)
    inverse = jnp.zeros((N_BLK,), jnp.int32).at[runs].set(jnp.arange(N_BLK, dtype=jnp.int32))
    slots = jnp.arange(PATCH_AMOUNT, dtype=jnp.int32)
    block = inverse[slots // BLK_DEV] * BLK_DEV + slots % BLK_DEV
    rows = jnp.arange(PATCH_CELL_HIGH, dtype=jnp.int32)
    cols = jnp.arange(PATCH_CELL_WIDE, dtype=jnp.int32)
    tile = block[:, None, None] * SUB + (rows // TY)[None, :, None] + 0 * cols[None, None, :]
    depth = jnp.minimum(LAYER_NUMBER, jax.random.randint(keys[0], (PATCH_AMOUNT, PATCH_CELL_HIGH, PATCH_CELL_WIDE), 1, 2 * LAYER_NUMBER))
    coast = jax.random.randint(keys[1], (PATCH_AMOUNT, PATCH_CELL_HIGH, PATCH_CELL_WIDE), 0, 10) == 0
    return jnp.where(coast | (live[tile] == 0), 0, depth).astype(jnp.int32)


def block_levels(key, shape, cuts, least, top_value):
    def one(dim, blocks):
        draws = jax.random.uniform(jax.random.fold_in(jax.random.fold_in(key, 6), dim), (blocks,), jnp.float32, least / len(cuts), top_value / len(cuts))
        return jnp.repeat(jnp.exp(draws), shape[dim] // blocks).reshape((-1,) + (1,) * (len(shape) - dim - 1))

    factor_of = one(*cuts[0])
    for cut in cuts[1:]:
        factor_of = factor_of * one(*cut)
    return factor_of


def centred(key, extent, scale, reach, cuts=(), held_as=jnp.bfloat16):
    array = jax.random.normal(key, extent, jnp.float32) * scale
    if len(cuts) > 0:
        array = block_levels(key, extent, cuts, -0.22, 0.18) * array
    return jnp.clip(array, min=-reach, max=reach).astype(held_as)


def setup_inputs(seed: int = 0, part: int = 0) -> dict:
    arg_keys = jax.random.split(jax.random.key(seed), 10)
    part_splits = jax.random.split(jax.random.fold_in(arg_keys[9], part), 10)
    return {
        "stack_wet_layers": draw_stack_wet_layers(jax.random.fold_in(jax.random.fold_in(arg_keys[9], part), 71), part),
        "patch_owner": draw_patch_owner(jax.random.fold_in(jax.random.fold_in(arg_keys[9], part), 71), part),
        "piece_owner": draw_piece_owner(jax.random.fold_in(jax.random.fold_in(arg_keys[9], part), 71), part),
        "piece_neighbours": draw_piece_neighbours(jax.random.fold_in(jax.random.fold_in(arg_keys[9], part), 71), part),
        "east_velocity": centred(part_splits[4], (PATCH_AMOUNT, LAYER_NUMBER, PATCH_CELL_HIGH, PATCH_CELL_WIDE), 1.0, 6.0, ((0, 16),), jnp.float32),
        "north_velocity": centred(part_splits[5], (PATCH_AMOUNT, LAYER_NUMBER, PATCH_CELL_HIGH, PATCH_CELL_WIDE), 1.0, 6.0, ((0, 16),), jnp.float32),
        "heat_anomaly": centred(part_splits[6], (PATCH_AMOUNT, LAYER_NUMBER, PATCH_CELL_HIGH, PATCH_CELL_WIDE), 1.0, 6.0, ((0, 16),), jnp.float32),
        "saltiness_anomaly": centred(part_splits[7], (PATCH_AMOUNT, LAYER_NUMBER, PATCH_CELL_HIGH, PATCH_CELL_WIDE), 1.0, 6.0, ((0, 16),), jnp.float32),
        "diffusivity_below": jnp.clip(jnp.exp(math.log(20.0) - 5.9914645 * jax.random.uniform(part_splits[8], (PATCH_AMOUNT, LAYER_NUMBER, PATCH_CELL_HIGH, PATCH_CELL_WIDE), jnp.float32) ** block_levels(part_splits[8], (PATCH_AMOUNT, LAYER_NUMBER, PATCH_CELL_HIGH, PATCH_CELL_WIDE), ((0, 16),), -0.2, 0.2)), 0.05, 20.0),
    }


NEIGHBOR_SIDES = ((-1, 0, 1.0), (1, 0, 1.0), (0, -1, 1.0), (0, 1, 1.0), (-1, -1, 0.25), (-1, 1, 0.25), (1, -1, 0.25), (1, 1, 0.25))
damping = 0.1
coriolis = 0.3
lowest = 0.02
highest = 2.0


def level_steps(count):
    return 1.0 + 0.1 * jnp.arange(count).astype(jnp.float32)


def stack_mixer(field, barotropic_linkage, iteration_number):
    levels = field.shape[1]
    zeros = jnp.zeros_like(field[:, 0])
    ratio = zeros
    value = zeros
    ratios = []
    values = []
    for level in range(levels):
        lower = barotropic_linkage[:, level - 1] if level > 0 else zeros
        upper = barotropic_linkage[:, level]
        denom = iteration_number[level] + lower + upper - lower * ratio
        value = (iteration_number[level] * field[:, level] + lower * value) / denom
        ratio = upper / denom
        ratios.append(ratio)
        values.append(value)
    current = values[levels - 1]
    result = [current]
    for level in range(levels - 2, -1, -1):
        current = values[level] + ratios[level] * current
        result.append(current)
    return jnp.stack(result[::-1], axis=1)


def internal_wave_part(stack_wet_layers, east_velocity, north_velocity, heat_anomaly, saltiness_anomaly, diffusivity_below):
    count = east_velocity.shape[1]
    iteration_number = level_steps(count)
    water_indicator = (jnp.arange(count)[None, :, None, None] < stack_wet_layers[:, None]).astype(jnp.float32)
    below = jnp.concatenate([water_indicator[:, 1:], jnp.zeros_like(water_indicator[:, :1])], axis=1)
    barotropic_linkage = diffusivity_below * below
    zonal_pred = water_indicator * (east_velocity + coriolis * north_velocity)
    meridional_pred = water_indicator * (north_velocity - coriolis * east_velocity)
    east_velocity_mixed = stack_mixer(zonal_pred, barotropic_linkage, iteration_number)
    north_velocity_mixed = stack_mixer(meridional_pred, barotropic_linkage, iteration_number)
    heat_anomaly_mixed = water_indicator * stack_mixer(heat_anomaly, 0.5 * barotropic_linkage, iteration_number)
    saltiness_mixed = water_indicator * stack_mixer(saltiness_anomaly, 0.5 * barotropic_linkage, iteration_number)
    total = jnp.sum(iteration_number)
    weights = iteration_number[None, :, None, None]
    transport_east = jnp.sum(weights * east_velocity_mixed, axis=1) / total
    transport_north = jnp.sum(weights * north_velocity_mixed, axis=1) / total
    layer_thickness_share = jnp.sum(weights * water_indicator, axis=1) / total
    return water_indicator, east_velocity_mixed, north_velocity_mixed, heat_anomaly_mixed, saltiness_mixed, transport_east, transport_north, layer_thickness_share


def to_tiles(field):
    count = field.shape[0]
    rows = field.shape[1] // SPLIT
    return field.reshape(count * SPLIT, rows, field.shape[2])


def from_tiles(tiles, count):
    return tiles.reshape(count, SPLIT * tiles.shape[1], tiles.shape[2])


def rim_of(field, width):
    count = field.shape[0]
    return jnp.concatenate([field[:, :width, :].reshape(count, -1), field[:, field.shape[1] - width:, :].reshape(count, -1), field[:, :, :width].reshape(count, -1), field[:, :, field.shape[2] - width:].reshape(count, -1)], axis=1)


def assemble(own, rims, width):
    count, rows, cols = own.shape
    edge = width * cols
    side = rows * width

    def top_of(which):
        return rims[:, which, :edge].reshape(count, width, cols)

    def bottom_of(which):
        return rims[:, which, edge:2 * edge].reshape(count, width, cols)

    def left_of(which):
        return rims[:, which, 2 * edge:2 * edge + side].reshape(count, rows, width)

    def right_of(which):
        return rims[:, which, 2 * edge + side:].reshape(count, rows, width)

    upper = jnp.concatenate([bottom_of(4)[:, :, cols - width:], bottom_of(0), bottom_of(5)[:, :, :width]], axis=2)
    middle = jnp.concatenate([right_of(2), own, left_of(3)], axis=2)
    lower = jnp.concatenate([top_of(6)[:, :, cols - width:], top_of(1), top_of(7)[:, :, :width]], axis=2)
    return jnp.concatenate([upper, middle, lower], axis=1)


def shifted(field, down, across):
    rows = field.shape[1]
    cols = field.shape[2]
    padded = jnp.pad(field, ((0, 0), (1, 1), (1, 1)))
    return padded[:, 1 + down:1 + down + rows, 1 + across:1 + across + cols]


def crop(field, width):
    return field[:, width:field.shape[1] - width, width:field.shape[2] - width]


def couplings(depth_pad):
    ocean = (depth_pad > 0).astype(jnp.float32)
    weights = []
    diagonal = damping + jnp.zeros_like(depth_pad)
    for down, across, factor in NEIGHBOR_SIDES:
        weight = factor * 0.5 * (depth_pad + shifted(depth_pad, down, across)) * ocean * shifted(ocean, down, across)
        weights.append(weight)
        diagonal = diagonal + weight
    return weights, diagonal, ocean


def apply_operator(field, weights, diagonal):
    result = diagonal * field
    for (down, across, factor), weight in zip(NEIGHBOR_SIDES, weights):
        result = result - weight * shifted(field, down, across)
    return result


def chebyshev_plan(count):
    centre = 0.5 * (highest + lowest)
    spread = 0.5 * (highest - lowest)
    sigma = centre / spread
    rho = 1.0 / sigma
    plan = []
    for step in range(count):
        fresh = 1.0 / (2.0 * sigma - rho)
        plan.append((fresh * rho, 2.0 * fresh / spread))
        rho = fresh
    return centre, plan


def group_rank(owner):
    total = owner.shape[0]
    order = jnp.argsort(owner, stable=True).astype(jnp.int32)
    ordered = owner[order]
    first = jnp.searchsorted(ordered, ordered, side="left").astype(jnp.int32)
    positions = jnp.arange(total).astype(jnp.int32) - first
    return jnp.zeros((total,), jnp.int32).at[order].set(positions)


def extend_all(field, piece_neighbours):
    rims = rim_of(field, 1)
    padded_rims = jnp.concatenate([rims, jnp.zeros((1, rims.shape[1]), rims.dtype)], axis=0)
    return assemble(field, padded_rims[piece_neighbours], 1)


def lone_patch(items):
    outputs = internal_wave_part(*[item[None] for item in items])
    return tuple(output[0] for output in outputs)


def reference(stack_wet_layers, patch_owner, piece_owner, piece_neighbours, east_velocity, north_velocity, heat_anomaly, saltiness_anomaly, diffusivity_below):
    water_indicator, east_velocity_mixed, north_velocity_mixed, heat_anomaly_mixed, saltiness_mixed, transport_east, transport_north, layer_thickness_share = lax.map(lone_patch, (stack_wet_layers, east_velocity, north_velocity, heat_anomaly, saltiness_anomaly, diffusivity_below))
    block_slot = patch_owner * BLK_DEV + group_rank(patch_owner)
    tile_ids = jnp.arange(NT).astype(jnp.int32)
    slot_tile = block_slot[tile_ids // SUB] * SUB + tile_ids % SUB
    live = (piece_owner >= 0).astype(jnp.float32)[:, None, None]
    zonal_tiles = to_tiles(transport_east)[slot_tile] * live
    north_tiles = to_tiles(transport_north)[slot_tile] * live
    depth_tiles = to_tiles(layer_thickness_share)[slot_tile] * live
    zonal_pad = extend_all(zonal_tiles, piece_neighbours)
    north_pad = extend_all(north_tiles, piece_neighbours)
    depth_pad = extend_all(depth_tiles, piece_neighbours)
    weights, diagonal, ocean = couplings(depth_pad)
    ocean_mid = crop(ocean, 1)
    diagonal_mid = crop(diagonal, 1)
    rows = zonal_tiles.shape[1]
    cols = zonal_tiles.shape[2]
    rhs = -(crop(zonal_pad, 1) - zonal_pad[:, 1:1 + rows, 0:cols] + crop(north_pad, 1) - north_pad[:, 0:rows, 1:1 + cols]) * ocean_mid
    centre, plan = chebyshev_plan(ITERS)
    height = jnp.zeros_like(rhs)
    resid = rhs
    search = resid / (centre * diagonal_mid)
    for step in range(ITERS):
        search_pad = extend_all(search, piece_neighbours)
        height = height + search
        resid = resid - crop(apply_operator(search_pad, weights, diagonal), 1)
        if step + 1 < ITERS:
            first, second = plan[step]
            search = first * search + second * resid / diagonal_mid
    height_pad = extend_all(height, piece_neighbours)
    east = (height_pad[:, 1:-1, 2:] - height) * ocean_mid * ocean[:, 1:-1, 2:]
    south = (height_pad[:, 2:, 1:-1] - height) * ocean_mid * ocean[:, 2:, 1:-1]
    tile_place = jnp.where(piece_owner >= 0, piece_owner * BT_DEV + group_rank(piece_owner), N_BLK * BT_DEV)
    sea_height_patches = jnp.zeros((N_BLK * BT_DEV, TY, TX), jnp.float32).at[tile_place].set(height, mode="drop")
    east_block = from_tiles(jnp.zeros_like(east).at[slot_tile].set(east), PATCH_AMOUNT)
    south_block = from_tiles(jnp.zeros_like(south).at[slot_tile].set(south), PATCH_AMOUNT)
    east_velocity_next = water_indicator * (east_velocity_mixed - east_block[:, None])
    north_velocity_next = water_indicator * (north_velocity_mixed - south_block[:, None])
    return east_velocity_next, north_velocity_next, heat_anomaly_mixed, saltiness_mixed, sea_height_patches
```

```python
import functools

import jax
import jax.numpy as jnp
from jax import lax
from jax.experimental import pallas as pl
from jax.experimental.pallas import tpu as pltpu
from jax.sharding import PartitionSpec as P

ITERS = 6
SUB = 4
BLK_DEV = 4
BT_DEV = 14
TILES_DEV = 16
LEVELS = 20
ROWS = 32
COLS = 128
TY = 8
STRIP = 16
PACK = 48

damping = 0.1
coriolis = 0.3
lowest = 0.02
highest = 2.0

STEPS = [1.0 + 0.1 * k for k in range(LEVELS)]
TOTAL = sum(STEPS)
MESH = pl.DeviceIdType.MESH


def chebyshev_plan(count):
    centre = 0.5 * (highest + lowest)
    spread = 0.5 * (highest - lowest)
    sigma = centre / spread
    rho = 1.0 / sigma
    plan = []
    for _ in range(count):
        fresh = 1.0 / (2.0 * sigma - rho)
        plan.append((fresh * rho, 2.0 * fresh / spread))
        rho = fresh
    return (centre, plan)


def lane_of(shape):
    return lax.broadcasted_iota(jnp.int32, shape, 1)


def row_of(shape):
    return lax.broadcasted_iota(jnp.int32, shape, 0)


def side_pack(field, edge):
    lane = lane_of((TY, COLS))
    out = jnp.zeros((TY, COLS), jnp.float32)
    for group in range(SUB):
        rows = field[group * TY : (group + 1) * TY]
        moved = pltpu.roll(rows, (16 + 32 * group) % COLS, 1)
        out = jnp.where(lane // 32 == group, moved, out)
        if edge is not None:
            moved = pltpu.roll(edge[group * TY : (group + 1) * TY], (1 + 32 * group) % COLS, 1)
            out = jnp.where(lane == 32 * group, moved, out)
    return out


def mix_kernel(
    wet_ref, u_ref, v_ref, t_ref, s_ref, k_ref,
    um_ref, vm_ref, tm_ref, sm_ref, div_ref, depth_ref, pack_ref,
    ratio_ref, half_ref, zonal_ref, north_ref,
):
    def strip(index, carry):
        rows = pl.ds(pl.multiple_of(index * STRIP, STRIP), STRIP)
        wet = wet_ref[rows, :]
        zero = jnp.zeros((STRIP, COLS), jnp.float32)
        lower = zero
        lower_half = zero
        ratio = zero
        ratio_half = zero
        mask = (wet > 0).astype(jnp.float32)
        depth = zero
        uv = vv = tv = sv = zero
        for k in range(LEVELS):
            step = STEPS[k]
            depth = depth + step * mask
            u = u_ref[k, rows, :]
            v = v_ref[k, rows, :]
            if k + 1 < LEVELS:
                below = (wet > k + 1).astype(jnp.float32)
                upper = k_ref[k, rows, :] * below
            else:
                below = zero
                upper = zero
            upper_half = 0.5 * upper
            inv = 1.0 / (step + upper + lower * (1.0 - ratio))
            inv_half = 1.0 / (step + upper_half + lower_half * (1.0 - ratio_half))
            scaled = step * mask
            uv = (scaled * (u + coriolis * v) + lower * uv) * inv
            vv = (scaled * (v - coriolis * u) + lower * vv) * inv
            tv = (step * t_ref[k, rows, :] + lower_half * tv) * inv_half
            sv = (step * s_ref[k, rows, :] + lower_half * sv) * inv_half
            ratio = upper * inv
            ratio_half = upper_half * inv_half
            um_ref[k, rows, :] = uv
            vm_ref[k, rows, :] = vv
            tm_ref[k, rows, :] = tv
            sm_ref[k, rows, :] = sv
            ratio_ref[k] = ratio
            half_ref[k] = ratio_half
            lower = upper
            lower_half = upper_half
            mask = below
        last = LEVELS - 1
        zonal = STEPS[last] * uv
        north = STEPS[last] * vv
        mask = (wet > last).astype(jnp.float32)
        tm_ref[last, rows, :] = tv * mask
        sm_ref[last, rows, :] = sv * mask
        for k in range(last - 1, -1, -1):
            ratio = ratio_ref[k]
            ratio_half = half_ref[k]
            uv = um_ref[k, rows, :] + ratio * uv
            vv = vm_ref[k, rows, :] + ratio * vv
            tv = tm_ref[k, rows, :] + ratio_half * tv
            sv = sm_ref[k, rows, :] + ratio_half * sv
            zonal = zonal + STEPS[k] * uv
            north = north + STEPS[k] * vv
            mask = (wet > k).astype(jnp.float32)
            um_ref[k, rows, :] = uv
            vm_ref[k, rows, :] = vv
            tm_ref[k, rows, :] = tv * mask
            sm_ref[k, rows, :] = sv * mask
        zonal_ref[rows, :] = zonal * (1.0 / TOTAL)
        north_ref[rows, :] = north * (1.0 / TOTAL)
        depth_ref[rows, :] = depth * (1.0 / TOTAL)
        return carry

    lax.fori_loop(0, ROWS // STRIP, strip, 0)
    zonal = zonal_ref[...]
    north = north_ref[...]
    depth = depth_ref[...]
    lane = lane_of((ROWS, COLS))
    row = row_of((ROWS, COLS))
    left = jnp.where(lane == 0, 0.0, pltpu.roll(zonal, 1, 1))
    above = jnp.where(row == 0, 0.0, pltpu.roll(north, 1, 0))
    div = zonal - left + north - above
    div_ref[...] = div
    pack_ref[0:8, :] = div[0:8]
    pack_ref[8:16, :] = div[24:32]
    pack_ref[8:9, :] = north[31:32]
    pack_ref[16:24, :] = side_pack(div, zonal)
    pack_ref[24:32, :] = depth[0:8]
    pack_ref[32:40, :] = depth[24:32]
    pack_ref[40:48, :] = side_pack(depth, None)


def column_mix(wet, u, v, t, s, kappa):
    blocks = u.shape[0]
    deep = pl.BlockSpec((None, LEVELS, ROWS, COLS), lambda i: (i, 0, 0, 0))
    flat = pl.BlockSpec((None, ROWS, COLS), lambda i: (i, 0, 0))
    deep_shape = jax.ShapeDtypeStruct(u.shape, jnp.float32)
    flat_shape = jax.ShapeDtypeStruct((blocks, ROWS, COLS), jnp.float32)
    return pl.pallas_call(
        mix_kernel,
        grid=(blocks,),
        in_specs=[flat] + [deep] * 5,
        out_specs=[deep] * 4 + [flat, flat, pl.BlockSpec((None, PACK, COLS), lambda i: (i, 0, 0))],
        out_shape=[deep_shape] * 4
        + [flat_shape, flat_shape, jax.ShapeDtypeStruct((blocks, PACK, COLS), jnp.float32)],
        scratch_shapes=[
            pltpu.VMEM((LEVELS, STRIP, COLS), jnp.float32),
            pltpu.VMEM((LEVELS, STRIP, COLS), jnp.float32),
            pltpu.VMEM((ROWS, COLS), jnp.float32),
            pltpu.VMEM((ROWS, COLS), jnp.float32),
        ],
        compiler_params=pltpu.CompilerParams(vmem_limit_bytes=32 * 2**20),
        name="column_mix",
    )(wet, u, v, t, s, kappa)


def greet(n, me):
    barrier = pltpu.get_barrier_semaphore()

    def one(k, carry):
        pl.semaphore_signal(
            barrier, inc=1, device_id={"blk": lax.rem(me + k, n)}, device_id_type=MESH
        )
        return carry

    lax.fori_loop(1, n, one, 0)
    pl.semaphore_wait(barrier, n - 1)


def gather_kernel(n, x_ref, out_ref, send_sem, recv_sem):
    me = lax.axis_index("blk")
    greet(n, me)

    def copy(k):
        return pltpu.make_async_remote_copy(
            src_ref=x_ref,
            dst_ref=out_ref.at[me],
            send_sem=send_sem.at[k],
            recv_sem=recv_sem.at[k],
            device_id={"blk": lax.rem(me + k, n)},
            device_id_type=MESH,
        )

    def begin(k, carry):
        copy(k).start()
        return carry

    def end(k, carry):
        copy(k).wait()
        return carry

    lax.fori_loop(1, n, begin, 0)
    out_ref[me] = x_ref[...]
    lax.fori_loop(1, n, end, 0)


def gather_packs(n, pack):
    shape = (n,) + pack.shape
    return pl.pallas_call(
        functools.partial(gather_kernel, n),
        out_shape=jax.ShapeDtypeStruct(shape, jnp.float32),
        in_specs=[pl.BlockSpec(memory_space=pltpu.VMEM)],
        out_specs=pl.BlockSpec(memory_space=pltpu.VMEM),
        scratch_shapes=[pltpu.SemaphoreType.DMA((n,)), pltpu.SemaphoreType.DMA((n,))],
        compiler_params=pltpu.CompilerParams(
            collective_id=0, has_side_effects=True, vmem_limit_bytes=32 * 2**20
        ),
        name="gather_packs",
    )(pack)


def spread_kernel(n, cap, place_ref, x_ref, out_ref, held, send_sem, recv_sem):
    me = lax.axis_index("blk")
    greet(n, me)

    def copy(k):
        other = lax.rem(me + k, n)
        return pltpu.make_async_remote_copy(
            src_ref=x_ref.at[other],
            dst_ref=held.at[me],
            send_sem=send_sem.at[k],
            recv_sem=recv_sem.at[k],
            device_id={"blk": other},
            device_id_type=MESH,
        )

    def begin(k, carry):
        copy(k).start()
        return carry

    def end(k, carry):
        copy(k).wait()
        return carry

    lax.fori_loop(1, n, begin, 0)
    held[me] = x_ref[me]
    lax.fori_loop(1, n, end, 0)
    for slot in range(BT_DEV):
        out_ref[slot] = held[place_ref[2 * slot], place_ref[2 * slot + 1]]


def spread_tiles(n, cap, place, tiles):
    return pl.pallas_call(
        functools.partial(spread_kernel, n, cap),
        out_shape=jax.ShapeDtypeStruct((BT_DEV, TY, COLS), jnp.float32),
        in_specs=[
            pl.BlockSpec(memory_space=pltpu.SMEM),
            pl.BlockSpec(memory_space=pltpu.VMEM),
        ],
        out_specs=pl.BlockSpec(memory_space=pltpu.VMEM),
        scratch_shapes=[
            pltpu.VMEM((n, cap, TY, COLS), jnp.float32),
            pltpu.SemaphoreType.DMA((n,)),
            pltpu.SemaphoreType.DMA((n,)),
        ],
        compiler_params=pltpu.CompilerParams(
            collective_id=1, has_side_effects=True, vmem_limit_bytes=32 * 2**20
        ),
        name="spread_tiles",
    )(place, tiles)


def sideways(main, side, amount):
    lane = lane_of(main.shape)
    edge = lane == (0 if amount == 1 else COLS - 1)
    rolled_main = pltpu.roll(main, amount % COLS, 1)
    rolled_side = pltpu.roll(side, amount % COLS, 1)
    return (
        jnp.where(edge, rolled_side, rolled_main),
        jnp.where(edge, rolled_main, rolled_side),
    )


def ring_sum(main, side):
    rows = main.shape[0]

    def vertical(field):
        return field + 0.25 * (pltpu.roll(field, 1, 0) + pltpu.roll(field, rows - 1, 0))

    vm = vertical(main)
    vs = vertical(side)
    lm, ls = sideways(vm, vs, 1)
    rm, rs = sideways(vm, vs, -1)
    return (
        4.0 * (vm - main) + (lm + rm),
        4.0 * (vs - side) + (ls + rs),
    )


def solve_kernel(
    n, cap, runs_ref, owner_ref, near_hbm, gathered, div_ref, depth_ref, wet_ref, um_ref, vm_ref,
    un_ref, vn_ref, out_ref, place_ref,
    near, scalars, counts, sem,
):
    step = pl.program_id(0)
    me = lax.axis_index("blk")

    @pl.when(step == 0)
    def _():
        def find(j, found):
            return jnp.where(runs_ref[j * BLK_DEV] == me, j, found)

        run = lax.fori_loop(0, n, find, 0)
        scalars[0] = run
        copy = pltpu.make_async_copy(
            near_hbm.at[pl.ds(pl.multiple_of(run * TILES_DEV, TILES_DEV), TILES_DEV)], near, sem
        )
        copy.start()

        def clear(j, carry):
            counts[j] = 0
            return carry

        lax.fori_loop(0, n, clear, 0)

        def scan(j, place):
            source = runs_ref[j * BLK_DEV]
            rank = 0
            for a in range(TILES_DEV):
                hit = (owner_ref[j * TILES_DEV + a] == me).astype(jnp.int32)
                place_ref[2 * place] = source
                place_ref[2 * place + 1] = rank
                place = place + hit
                rank = jnp.minimum(rank + hit, cap - 1)
            return place

        lax.fori_loop(0, n, scan, 0)
        copy.wait()

    run = scalars[0]
    base = step * SUB

    def where_is(tile):
        block = tile // SUB
        there = block < n * BLK_DEV
        safe = jnp.where(there, block, 0)
        return (runs_ref[safe], safe % BLK_DEV, there.astype(jnp.float32))

    above = where_is(near[base, 0])
    below = where_is(near[base + SUB - 1, 1])
    above_left = where_is(near[base, 4])
    above_right = where_is(near[base, 5])
    below_left = where_is(near[base + SUB - 1, 6])
    below_right = where_is(near[base + SUB - 1, 7])
    left_tile = near[base, 2]
    right_tile = near[base, 3]
    for a in range(1, SUB):
        left_tile = jnp.minimum(left_tile, near[base + a, 2])
        right_tile = jnp.minimum(right_tile, near[base + a, 3])
    left = where_is(left_tile)
    right = where_is(right_tile)
    own = (me, step, jnp.float32(1.0))

    def load(who, start, rows=TY):
        device, slot, there = who
        return gathered[device, slot, start : start + rows, :] * there

    lane8 = lane_of((TY, COLS))
    row8 = row_of((TY, COLS))

    def corner(who_left, who_right, start):
        mixed = jnp.where(lane8 < TY, load(who_right, start), load(who_left, start))
        return jnp.where((lane8 < TY) | (lane8 >= COLS - TY), mixed, 0.0)

    def beside(start):
        packed = jnp.where(lane8 % 32 >= 16, load(right, start), load(left, start))
        parts = []
        for group in range(SUB):
            moved = pltpu.roll(packed, (112 - 32 * group) % COLS, 1)
            parts.append(jnp.where((lane8 < TY) | (lane8 >= COLS - TY), moved, 0.0))
        return parts

    def edge_column(upper, middle, lower):
        packed = load(middle, 16)
        parts = [pltpu.roll(load(upper, 16), 32, 1)]
        for group in range(SUB):
            moved = packed if group == 0 else pltpu.roll(packed, COLS - 32 * group, 1)
            parts.append(moved)
        parts.append(load(lower, 16))
        return jnp.where(lane48 == 0, jnp.concatenate(parts, axis=0), 0.0)

    lane48 = lane_of((PACK, COLS))
    depth_main = jnp.concatenate([load(above, 32), depth_ref[...], load(below, 24)], axis=0)
    depth_side = jnp.concatenate(
        [corner(above_left, above_right, 32)] + beside(40) + [corner(below_left, below_right, 24)],
        axis=0,
    )
    top_main = load(above, 8)
    top_side = corner(above_left, above_right, 8)
    first_row = row8 == 0
    mid_main = div_ref[...]
    mid_side = beside(16)
    own_main = mid_main[0:8] - jnp.where(first_row, top_main, 0.0)
    mid_side[0] = mid_side[0] - jnp.where(first_row, top_side, 0.0)
    low_main = load(below, 0) - jnp.where(first_row, load(own, 8), 0.0)
    low_side = corner(below_left, below_right, 0) - jnp.where(
        first_row, corner(left, right, 8), 0.0
    )
    div_main = jnp.concatenate([top_main, own_main, mid_main[8:], low_main], axis=0)
    div_side = jnp.concatenate([top_side] + mid_side + [low_side], axis=0)
    div_main = div_main - edge_column(above_left, left, below_left)
    div_side = div_side - edge_column(above, own, below)

    centre, plan = chebyshev_plan(ITERS)
    depths = (depth_main, depth_side)
    divs = (div_main, div_side)
    ocean = [(d > 0).astype(jnp.float32) for d in depths]
    near_ocean = ring_sum(*ocean)
    near_depth = ring_sum(*depths)
    half = [0.5 * o for o in ocean]
    diagonal = [
        damping + h * (d * a + b) for h, d, a, b in zip(half, depths, near_ocean, near_depth)
    ]
    inverse = [1.0 / x for x in diagonal]
    resid = [-(x * o) for x, o in zip(divs, ocean)]
    search = [r * i * (1.0 / centre) for r, i in zip(resid, inverse)]
    height = [search[0], search[1]]
    for it in range(ITERS - 1):
        around = ring_sum(*search)
        weighted = ring_sum(*[d * s for d, s in zip(depths, search)])
        resid = [
            r - (g * s - h * (d * a + b))
            for r, g, s, h, d, a, b in zip(
                resid, diagonal, search, half, depths, around, weighted
            )
        ]
        first, second = plan[it]
        search = [first * s + second * r * i for s, r, i in zip(search, resid, inverse)]
        height = [e + s for e, s in zip(height, search)]
    eta = height[0][TY : TY + ROWS]
    ocean_mid = ocean[0][TY : TY + ROWS]
    eta_east = sideways(height[0], height[1], -1)[0][TY : TY + ROWS]
    ocean_east = sideways(ocean[0], ocean[1], -1)[0][TY : TY + ROWS]
    eta_south = pltpu.roll(height[0], PACK - 1, 0)[TY : TY + ROWS]
    ocean_south = pltpu.roll(ocean[0], PACK - 1, 0)[TY : TY + ROWS]
    east = (eta_east - eta) * ocean_mid * ocean_east
    south = (eta_south - eta) * ocean_mid * ocean_south

    for a in range(SUB):
        target = owner_ref[run * TILES_DEV + base + a]

        @pl.when(target >= 0)
        def _():
            rank = counts[target]
            counts[target] = rank + 1
            out_ref[target, rank] = eta[a * TY : (a + 1) * TY]

    wet = wet_ref[...]
    for k in range(LEVELS):
        wetted = wet > k
        un_ref[k] = jnp.where(wetted, um_ref[k] - east, 0.0)
        vn_ref[k] = jnp.where(wetted, vm_ref[k] - south, 0.0)


def solve(n, cap, patch_owner, piece_owner, neighbours, gathered, div, depth, wet, um, vm):
    blocks = um.shape[0]
    deep = pl.BlockSpec((None, LEVELS, ROWS, COLS), lambda i: (i, 0, 0, 0))
    flat = pl.BlockSpec((None, ROWS, COLS), lambda i: (i, 0, 0))
    deep_shape = jax.ShapeDtypeStruct(um.shape, jnp.float32)
    smem = pl.BlockSpec(memory_space=pltpu.SMEM)
    return pl.pallas_call(
        functools.partial(solve_kernel, n, cap),
        grid=(blocks,),
        in_specs=[
            smem,
            smem,
            pl.BlockSpec(memory_space=pl.ANY),
            pl.BlockSpec(gathered.shape, lambda i: (0, 0, 0, 0)),
            flat,
            flat,
            flat,
            deep,
            deep,
        ],
        out_specs=[deep, deep, pl.BlockSpec((n, cap, TY, COLS), lambda i: (0, 0, 0, 0)), smem],
        out_shape=[
            deep_shape,
            deep_shape,
            jax.ShapeDtypeStruct((n, cap, TY, COLS), jnp.float32),
            jax.ShapeDtypeStruct((2 * BT_DEV + 4,), jnp.int32),
        ],
        scratch_shapes=[
            pltpu.SMEM((TILES_DEV, 8), jnp.int32),
            pltpu.SMEM((1,), jnp.int32),
            pltpu.SMEM((n,), jnp.int32),
            pltpu.SemaphoreType.DMA,
        ],
        compiler_params=pltpu.CompilerParams(vmem_limit_bytes=48 * 2**20),
        name="solve",
    )(patch_owner, piece_owner, neighbours, gathered, div, depth, wet, um, vm)


def on_device(n, wet, patch_owner, piece_owner, neighbours, u, v, t, s, kappa):
    cap = max(2, TILES_DEV // n)
    um, vm, tm, sm, div, depth, pack = column_mix(wet, u, v, t, s, kappa)
    gathered = gather_packs(n, pack)
    un, vn, tiles, place = solve(
        n, cap, patch_owner, piece_owner, neighbours, gathered, div, depth, wet, um, vm
    )
    height = spread_tiles(n, cap, place, tiles)
    return (un, vn, tm, sm, height)


def solution(mesh):
    deep = P(("group", "blk"), None, None, None)
    flat = P(("group", "blk"), None, None)
    return jax.shard_map(
        functools.partial(on_device, mesh.shape["blk"]),
        mesh=mesh,
        in_specs=(flat, P("group"), P("group"), P("group", None)) + (deep,) * 5,
        out_specs=(deep,) * 4 + (flat,),
        check_vma=False,
    )
```

```python
import functools

import jax
import jax.numpy as jnp
from jax import lax
from jax.experimental import pallas as pl
from jax.experimental.pallas import tpu as pltpu
from jax.sharding import PartitionSpec as P

ITERS = 6
SUB = 4
BLK_DEV = 4
BT_DEV = 14
TILES_DEV = 16
LEVELS = 20
ROWS = 32
COLS = 128
TY = 8
STRIP = 16
PACK = 24
TALL = 48

damping = 0.1
coriolis = 0.3
lowest = 0.02
highest = 2.0

STEPS = [1.0 + 0.1 * k for k in range(LEVELS)]
TOTAL = sum(STEPS)
MESH = pl.DeviceIdType.MESH


def chebyshev_plan(count):
    centre = 0.5 * (highest + lowest)
    spread = 0.5 * (highest - lowest)
    sigma = centre / spread
    rho = 1.0 / sigma
    plan = []
    for _ in range(count):
        fresh = 1.0 / (2.0 * sigma - rho)
        plan.append((fresh * rho, 2.0 * fresh / spread))
        rho = fresh
    return (centre, plan)


def lane_of(shape):
    return lax.broadcasted_iota(jnp.int32, shape, 1)


def row_of(shape):
    return lax.broadcasted_iota(jnp.int32, shape, 0)


def side_pack(field, edge):
    lane = lane_of((TY, COLS))
    out = jnp.zeros((TY, COLS), jnp.float32)
    for group in range(SUB):
        rows = field[group * TY : (group + 1) * TY]
        moved = pltpu.roll(rows, (16 + 32 * group) % COLS, 1)
        out = jnp.where(lane // 32 == group, moved, out)
        if edge is not None:
            moved = pltpu.roll(edge[group * TY : (group + 1) * TY], (1 + 32 * group) % COLS, 1)
            out = jnp.where(lane == 32 * group, moved, out)
    return out


def scalars_mix_kernel(wet_ref, t_ref, s_ref, k_ref, tm_ref, sm_ref, half_ref):
    def strip(index, carry):
        rows = pl.ds(pl.multiple_of(index * STRIP, STRIP), STRIP)
        wet = wet_ref[rows, :]
        zero = jnp.zeros((STRIP, COLS), jnp.float32)
        lower = ratio = tv = sv = zero
        for k in range(LEVELS):
            step = STEPS[k]
            if k + 1 < LEVELS:
                upper = jnp.where(wet > k + 1, 0.5 * k_ref[k, rows, :], 0.0)
            else:
                upper = zero
            inv = 1.0 / (step + upper + lower * (1.0 - ratio))
            tv = (step * t_ref[k, rows, :] + lower * tv) * inv
            sv = (step * s_ref[k, rows, :] + lower * sv) * inv
            ratio = upper * inv
            tm_ref[k, rows, :] = tv
            sm_ref[k, rows, :] = sv
            half_ref[k] = ratio
            lower = upper
        last = LEVELS - 1
        tm_ref[last, rows, :] = jnp.where(wet > last, tv, 0.0)
        sm_ref[last, rows, :] = jnp.where(wet > last, sv, 0.0)
        for k in range(last - 1, -1, -1):
            ratio = half_ref[k]
            tv = tm_ref[k, rows, :] + ratio * tv
            sv = sm_ref[k, rows, :] + ratio * sv
            tm_ref[k, rows, :] = jnp.where(wet > k, tv, 0.0)
            sm_ref[k, rows, :] = jnp.where(wet > k, sv, 0.0)
        return carry

    lax.fori_loop(0, ROWS // STRIP, strip, 0)


def scalars_mix(wet, t, s, kappa):
    blocks = t.shape[0]
    deep = pl.BlockSpec((None, LEVELS, ROWS, COLS), lambda i: (i, 0, 0, 0))
    flat = pl.BlockSpec((None, ROWS, COLS), lambda i: (i, 0, 0))
    return pl.pallas_call(
        scalars_mix_kernel,
        grid=(blocks,),
        in_specs=[flat, deep, deep, deep],
        out_specs=[deep, deep],
        out_shape=[jax.ShapeDtypeStruct(t.shape, jnp.float32)] * 2,
        scratch_shapes=[pltpu.VMEM((LEVELS, STRIP, COLS), jnp.float32)],
        compiler_params=pltpu.CompilerParams(vmem_limit_bytes=24 * 2**20),
        name="scalars_mix",
    )(wet, t, s, kappa)


def greet(n, me):
    barrier = pltpu.get_barrier_semaphore()

    def one(k, carry):
        pl.semaphore_signal(
            barrier, inc=1, device_id={"blk": lax.rem(me + k, n)}, device_id_type=MESH
        )
        return carry

    lax.fori_loop(1, n, one, 0)
    pl.semaphore_wait(barrier, n - 1)


class Relay:
    def __init__(self, n, me, x_ref, out_ref, send_sem, recv_sem):
        self.me, self.x, self.out = me, x_ref, out_ref
        self.send_sem, self.recv_sem = send_sem, recv_sem
        self.sent = []
        depth = n // 4
        z, y, c = me // 4, (me // 2) % 2, me % 2

        def at(z, y, c):
            return (z * 2 + y) * 2 + c

        hops = sorted(range(1, depth), key=lambda k: min(k, depth - k))
        far = [lax.rem(z + k, depth) for k in hops]
        self.line = [at(f, y, c) for f in far]
        self.y_peer = at(z, 1 - y, c)
        self.sibling = at(z, y, 1 - c)
        self.cross = [self.y_peer] + [at(f, 1 - y, c) for f in far]
        self.rest = [self.sibling] + [at(f, y, 1 - c) for f in far]
        self.rest += [at(f, 1 - y, 1 - c) for f in [z] + far]
        self.peers = self.line + [self.y_peer, self.sibling]

    def copy(self, source, device, slot, first):
        return pltpu.make_async_remote_copy(
            src_ref=self.x if first else self.out.at[source],
            dst_ref=self.out.at[source],
            send_sem=self.send_sem.at[slot],
            recv_sem=self.recv_sem.at[source],
            device_id={"blk": device},
            device_id_type=MESH,
        )

    def send(self, source, device, first=False):
        copy = self.copy(source, device, len(self.sent), first)
        copy.start()
        self.sent.append(copy)

    def arrived(self, source):
        self.copy(source, self.sibling, 0, False).wait_recv()

    def start(self):
        for peer in self.peers:
            self.send(self.me, peer, True)
        self.out[self.me] = self.x[...]

    def second(self):
        for source in self.line:
            self.arrived(source)
            self.send(source, self.y_peer)
            self.send(source, self.sibling)

    def third(self):
        for source in self.cross:
            self.arrived(source)
            self.send(source, self.sibling)

    def finish(self):
        for source in self.rest:
            self.arrived(source)
        for copy in self.sent:
            copy.wait_send()


def flow_kernel(
    n, wet_hbm, u_hbm, v_hbm, k_hbm,
    um_ref, vm_ref, div_ref, depth_ref, got_div, got_depth,
    wet_ref, u_ref, v_ref, k_ref, ratio_ref, zonal_ref, north_ref, div_pack, depth_pack,
    wet_sem, u_sem, v_sem, k_sem, div_send, div_recv, depth_send, depth_recv,
):
    me = lax.axis_index("blk")
    relay_depth = Relay(n, me, depth_pack, got_depth, depth_send, depth_recv)
    relay_div = Relay(n, me, div_pack, got_div, div_send, div_recv)
    barrier = pltpu.get_barrier_semaphore()
    for peer in relay_depth.peers:
        pl.semaphore_signal(barrier, inc=1, device_id={"blk": peer}, device_id_type=MESH)
    wet_copy = pltpu.make_async_copy(wet_hbm, wet_ref, wet_sem)
    wet_copy.start()

    def fetch(block):
        return [
            pltpu.make_async_copy(hbm.at[block], ref.at[block], sem.at[block])
            for hbm, ref, sem in ((u_hbm, u_ref, u_sem), (v_hbm, v_ref, v_sem), (k_hbm, k_ref, k_sem))
        ]

    for block in range(BLK_DEV):
        for copy in fetch(block):
            copy.start()
    wet_copy.wait()
    for block in range(BLK_DEV):
        count = wet_ref[block].astype(jnp.float32)
        depth = (count + 0.05 * (count * (count - 1.0))) * (1.0 / TOTAL)
        depth_ref[block] = depth
        depth_pack[block, 0:8] = depth[0:8]
        depth_pack[block, 8:16] = depth[24:32]
        depth_pack[block, 16:24] = side_pack(depth, None)
    pl.semaphore_wait(barrier, len(relay_depth.peers))
    relay_depth.start()

    def one_block(block, carry):
        for copy in fetch(block):
            copy.wait()

        def strip(index, inner):
            rows = pl.ds(pl.multiple_of(index * STRIP, STRIP), STRIP)
            wet = wet_ref[block, rows, :]
            zero = jnp.zeros((STRIP, COLS), jnp.float32)
            lower = ratio = uv = vv = zero
            for k in range(LEVELS):
                step = STEPS[k]
                u = u_ref[block, k, rows, :]
                v = v_ref[block, k, rows, :]
                if k + 1 < LEVELS:
                    upper = jnp.where(wet > k + 1, k_ref[block, k, rows, :], 0.0)
                else:
                    upper = zero
                inv = 1.0 / (step + upper + lower * (1.0 - ratio))
                scaled = jnp.where(wet > k, step, 0.0)
                uv = (scaled * (u + coriolis * v) + lower * uv) * inv
                vv = (scaled * (v - coriolis * u) + lower * vv) * inv
                ratio = upper * inv
                um_ref[block, k, rows, :] = uv
                vm_ref[block, k, rows, :] = vv
                ratio_ref[k] = ratio
                lower = upper
            last = LEVELS - 1
            zonal = STEPS[last] * uv
            north = STEPS[last] * vv
            for k in range(last - 1, -1, -1):
                ratio = ratio_ref[k]
                uv = um_ref[block, k, rows, :] + ratio * uv
                vv = vm_ref[block, k, rows, :] + ratio * vv
                zonal = zonal + STEPS[k] * uv
                north = north + STEPS[k] * vv
                um_ref[block, k, rows, :] = uv
                vm_ref[block, k, rows, :] = vv
            zonal_ref[rows, :] = zonal * (1.0 / TOTAL)
            north_ref[rows, :] = north * (1.0 / TOTAL)
            return inner

        lax.fori_loop(0, ROWS // STRIP, strip, 0)
        zonal = zonal_ref[...]
        north = north_ref[...]
        lane = lane_of((ROWS, COLS))
        row = row_of((ROWS, COLS))
        left = jnp.where(lane == 0, 0.0, pltpu.roll(zonal, 1, 1))
        above = jnp.where(row == 0, 0.0, pltpu.roll(north, 1, 0))
        div = zonal - left + north - above
        div_ref[block] = div
        div_pack[block, 0:8] = div[0:8]
        div_pack[block, 8:16] = jnp.where(
            row_of((TY, COLS)) == 0, pltpu.roll(north[24:32], 1, 0), div[24:32]
        )
        div_pack[block, 16:24] = side_pack(div, zonal)
        return carry

    lax.fori_loop(0, BLK_DEV, one_block, 0)
    relay_div.start()
    relay_depth.second()
    relay_depth.third()
    relay_div.second()
    relay_div.third()
    relay_depth.finish()
    relay_div.finish()


def flow(n, wet, u, v, kappa):
    blocks = u.shape[0]
    deep = jax.ShapeDtypeStruct(u.shape, jnp.float32)
    flat = jax.ShapeDtypeStruct((blocks, ROWS, COLS), jnp.float32)
    got = jax.ShapeDtypeStruct((n, blocks, PACK, COLS), jnp.float32)
    vmem = pl.BlockSpec(memory_space=pltpu.VMEM)
    hbm = pl.BlockSpec(memory_space=pltpu.MemorySpace.HBM)
    pack = pltpu.VMEM((blocks, PACK, COLS), jnp.float32)
    return pl.pallas_call(
        functools.partial(flow_kernel, n),
        in_specs=[hbm] * 4,
        out_specs=[vmem] * 6,
        out_shape=[deep, deep, flat, flat, got, got],
        scratch_shapes=[
            pltpu.VMEM(wet.shape, jnp.int32),
            pltpu.VMEM(u.shape, jnp.float32),
            pltpu.VMEM(u.shape, jnp.float32),
            pltpu.VMEM(u.shape, jnp.float32),
            pltpu.VMEM((LEVELS, STRIP, COLS), jnp.float32),
            pltpu.VMEM((ROWS, COLS), jnp.float32),
            pltpu.VMEM((ROWS, COLS), jnp.float32),
            pack,
            pack,
            pltpu.SemaphoreType.DMA,
        ]
        + [pltpu.SemaphoreType.DMA((blocks,))] * 3
        + [pltpu.SemaphoreType.DMA((n,))] * 4,
        compiler_params=pltpu.CompilerParams(
            collective_id=0, has_side_effects=True, vmem_limit_bytes=28 * 2**20
        ),
        name="flow",
    )(wet, u, v, kappa)


def spread_kernel(n, cap, place_ref, x_ref, out_ref, held, send_sem, recv_sem):
    me = lax.axis_index("blk")
    greet(n, me)

    def copy(k):
        other = lax.rem(me + k, n)
        return pltpu.make_async_remote_copy(
            src_ref=x_ref.at[other],
            dst_ref=held.at[me],
            send_sem=send_sem.at[k],
            recv_sem=recv_sem.at[k],
            device_id={"blk": other},
            device_id_type=MESH,
        )

    def begin(k, carry):
        copy(k).start()
        return carry

    def end(k, carry):
        copy(k).wait()
        return carry

    lax.fori_loop(1, n, begin, 0)
    held[me] = x_ref[me]
    lax.fori_loop(1, n, end, 0)
    for slot in range(BT_DEV):
        out_ref[slot] = held[place_ref[2 * slot], place_ref[2 * slot + 1]]


def spread_tiles(n, cap, place, tiles):
    return pl.pallas_call(
        functools.partial(spread_kernel, n, cap),
        out_shape=jax.ShapeDtypeStruct((BT_DEV, TY, COLS), jnp.float32),
        in_specs=[
            pl.BlockSpec(memory_space=pltpu.SMEM),
            pl.BlockSpec(memory_space=pltpu.VMEM),
        ],
        out_specs=pl.BlockSpec(memory_space=pltpu.VMEM),
        scratch_shapes=[
            pltpu.VMEM((n, cap, TY, COLS), jnp.float32),
            pltpu.SemaphoreType.DMA((n,)),
            pltpu.SemaphoreType.DMA((n,)),
        ],
        compiler_params=pltpu.CompilerParams(
            collective_id=1, has_side_effects=True, vmem_limit_bytes=32 * 2**20
        ),
        name="spread_tiles",
    )(place, tiles)


def sideways(main, side, amount):
    lane = lane_of(main.shape)
    edge = lane == (0 if amount == 1 else COLS - 1)
    rolled_main = pltpu.roll(main, amount % COLS, 1)
    rolled_side = pltpu.roll(side, amount % COLS, 1)
    return (
        jnp.where(edge, rolled_side, rolled_main),
        jnp.where(edge, rolled_main, rolled_side),
    )


def ring_sum(main, side):
    rows = main.shape[0]

    def vertical(field):
        return field + 0.25 * (pltpu.roll(field, 1, 0) + pltpu.roll(field, rows - 1, 0))

    vm = vertical(main)
    vs = vertical(side)
    lm, ls = sideways(vm, vs, 1)
    rm, rs = sideways(vm, vs, -1)
    return (
        4.0 * (vm - main) + (lm + rm),
        4.0 * (vs - side) + (ls + rs),
    )


def solve_kernel(
    n, cap, runs_ref, owner_ref, near, got_div, got_depth, div_ref, depth_ref, wet_ref, um_ref, vm_ref,
    un_ref, vn_ref, out_ref, place_ref,
    scalars, counts,
):
    step = pl.program_id(0)
    me = lax.axis_index("blk")

    @pl.when(step == 0)
    def _():
        def find(j, found):
            return jnp.where(runs_ref[j * BLK_DEV] == me, j, found)

        run = lax.fori_loop(0, n, find, 0)
        scalars[0] = run
        def clear(j, carry):
            counts[j] = 0
            return carry

        lax.fori_loop(0, n, clear, 0)

        def scan(j, place):
            source = runs_ref[j * BLK_DEV]
            rank = 0
            for a in range(TILES_DEV):
                hit = (owner_ref[j * TILES_DEV + a] == me).astype(jnp.int32)
                place_ref[2 * place] = source
                place_ref[2 * place + 1] = rank
                place = place + hit
                rank = jnp.minimum(rank + hit, cap - 1)
            return place

        lax.fori_loop(0, n, scan, 0)

    run = scalars[0]
    base = step * SUB

    def where_is(tile):
        block = tile // SUB
        there = block < n * BLK_DEV
        safe = jnp.where(there, block, 0)
        return (runs_ref[safe], safe % BLK_DEV, there.astype(jnp.float32))

    first = run * TILES_DEV + base
    final = first + SUB - 1
    above = where_is(near[0, first])
    below = where_is(near[1, final])
    above_left = where_is(near[4, first])
    above_right = where_is(near[5, first])
    below_left = where_is(near[6, final])
    below_right = where_is(near[7, final])
    left_tile = near[2, first]
    right_tile = near[3, first]
    for a in range(1, SUB):
        left_tile = jnp.minimum(left_tile, near[2, first + a])
        right_tile = jnp.minimum(right_tile, near[3, first + a])
    left = where_is(left_tile)
    right = where_is(right_tile)
    own = (me, step, jnp.float32(1.0))

    def load(got, who, start):
        device, slot, there = who
        return got[device, slot, start : start + TY, :] * there

    lane8 = lane_of((TY, COLS))
    row8 = row_of((TY, COLS))

    def corner(got, who_left, who_right, start):
        mixed = jnp.where(lane8 < TY, load(got, who_right, start), load(got, who_left, start))
        return jnp.where((lane8 < TY) | (lane8 >= COLS - TY), mixed, 0.0)

    def beside(got):
        packed = jnp.where(lane8 % 32 >= 16, load(got, right, 16), load(got, left, 16))
        parts = []
        for group in range(SUB):
            moved = pltpu.roll(packed, (112 - 32 * group) % COLS, 1)
            parts.append(jnp.where((lane8 < TY) | (lane8 >= COLS - TY), moved, 0.0))
        return parts

    def edge_column(upper, middle, lower):
        packed = load(got_div, middle, 16)
        parts = [pltpu.roll(load(got_div, upper, 16), 32, 1)]
        for group in range(SUB):
            moved = packed if group == 0 else pltpu.roll(packed, COLS - 32 * group, 1)
            parts.append(moved)
        parts.append(load(got_div, lower, 16))
        return jnp.where(lane48 == 0, jnp.concatenate(parts, axis=0), 0.0)

    lane48 = lane_of((TALL, COLS))
    depth_main = jnp.concatenate(
        [load(got_depth, above, 8), depth_ref[...], load(got_depth, below, 0)], axis=0
    )
    depth_side = jnp.concatenate(
        [corner(got_depth, above_left, above_right, 8)]
        + beside(got_depth)
        + [corner(got_depth, below_left, below_right, 0)],
        axis=0,
    )
    top_main = load(got_div, above, 8)
    top_side = corner(got_div, above_left, above_right, 8)
    first_row = row8 == 0
    mid_main = div_ref[...]
    mid_side = beside(got_div)
    own_main = mid_main[0:8] - jnp.where(first_row, top_main, 0.0)
    mid_side[0] = mid_side[0] - jnp.where(first_row, top_side, 0.0)
    low_main = load(got_div, below, 0) - jnp.where(first_row, load(got_div, own, 8), 0.0)
    low_side = corner(got_div, below_left, below_right, 0) - jnp.where(
        first_row, corner(got_div, left, right, 8), 0.0
    )
    div_main = jnp.concatenate([top_main, own_main, mid_main[8:], low_main], axis=0)
    div_side = jnp.concatenate([top_side] + mid_side + [low_side], axis=0)
    div_main = div_main - edge_column(above_left, left, below_left)
    div_side = div_side - edge_column(above, own, below)

    centre, plan = chebyshev_plan(ITERS)
    depths = (depth_main, depth_side)
    divs = (div_main, div_side)
    ocean = [(d > 0).astype(jnp.float32) for d in depths]
    near_ocean = ring_sum(*ocean)
    near_depth = ring_sum(*depths)
    half = [0.5 * o for o in ocean]
    diagonal = [
        damping + h * (d * a + b) for h, d, a, b in zip(half, depths, near_ocean, near_depth)
    ]
    inverse = [1.0 / x for x in diagonal]
    resid = [-(x * o) for x, o in zip(divs, ocean)]
    search = [r * i * (1.0 / centre) for r, i in zip(resid, inverse)]
    height = [search[0], search[1]]
    for it in range(ITERS - 1):
        around = ring_sum(*search)
        weighted = ring_sum(*[d * s for d, s in zip(depths, search)])
        resid = [
            r - (g * s - h * (d * a + b))
            for r, g, s, h, d, a, b in zip(
                resid, diagonal, search, half, depths, around, weighted
            )
        ]
        first, second = plan[it]
        search = [first * s + second * r * i for s, r, i in zip(search, resid, inverse)]
        height = [e + s for e, s in zip(height, search)]
    eta = height[0][TY : TY + ROWS]
    ocean_mid = ocean[0][TY : TY + ROWS]
    eta_east = sideways(height[0], height[1], -1)[0][TY : TY + ROWS]
    ocean_east = sideways(ocean[0], ocean[1], -1)[0][TY : TY + ROWS]
    eta_south = pltpu.roll(height[0], TALL - 1, 0)[TY : TY + ROWS]
    ocean_south = pltpu.roll(ocean[0], TALL - 1, 0)[TY : TY + ROWS]
    east = (eta_east - eta) * ocean_mid * ocean_east
    south = (eta_south - eta) * ocean_mid * ocean_south

    for a in range(SUB):
        target = owner_ref[run * TILES_DEV + base + a]

        @pl.when(target >= 0)
        def _():
            rank = counts[target]
            counts[target] = rank + 1
            out_ref[target, rank] = eta[a * TY : (a + 1) * TY]

    wet = wet_ref[...]
    for k in range(LEVELS):
        wetted = wet > k
        un_ref[k] = jnp.where(wetted, um_ref[k] - east, 0.0)
        vn_ref[k] = jnp.where(wetted, vm_ref[k] - south, 0.0)


def solve(n, cap, patch_owner, piece_owner, near, got_div, got_depth, div, depth, wet, um, vm):
    blocks = um.shape[0]
    deep = pl.BlockSpec((None, LEVELS, ROWS, COLS), lambda i: (i, 0, 0, 0))
    flat = pl.BlockSpec((None, ROWS, COLS), lambda i: (i, 0, 0))
    deep_shape = jax.ShapeDtypeStruct(um.shape, jnp.float32)
    smem = pl.BlockSpec(memory_space=pltpu.SMEM)
    return pl.pallas_call(
        functools.partial(solve_kernel, n, cap),
        grid=(blocks,),
        in_specs=[
            smem,
            smem,
            smem,
            pl.BlockSpec(memory_space=pltpu.VMEM),
            pl.BlockSpec(memory_space=pltpu.VMEM),
            flat,
            flat,
            flat,
            deep,
            deep,
        ],
        out_specs=[deep, deep, pl.BlockSpec((n, cap, TY, COLS), lambda i: (0, 0, 0, 0)), smem],
        out_shape=[
            deep_shape,
            deep_shape,
            jax.ShapeDtypeStruct((n, cap, TY, COLS), jnp.float32),
            jax.ShapeDtypeStruct((2 * BT_DEV + 4,), jnp.int32),
        ],
        scratch_shapes=[
            pltpu.SMEM((1,), jnp.int32),
            pltpu.SMEM((n,), jnp.int32),
        ],
        compiler_params=pltpu.CompilerParams(vmem_limit_bytes=48 * 2**20),
        name="solve",
    )(patch_owner, piece_owner, near, got_div, got_depth, div, depth, wet, um, vm)


def on_device(n, wet, patch_owner, piece_owner, neighbours, u, v, t, s, kappa):
    cap = max(2, TILES_DEV // n)
    um, vm, div, depth, got_div, got_depth = flow(n, wet, u, v, kappa)
    tm, sm = scalars_mix(wet, t, s, kappa)
    un, vn, tiles, place = solve(
        n, cap, patch_owner, piece_owner, neighbours.T,
        got_div, got_depth, div, depth, wet, um, vm,
    )
    height = spread_tiles(n, cap, place, tiles)
    return (un, vn, tm, sm, height)


def solution(mesh):
    deep = P(("group", "blk"), None, None, None)
    flat = P(("group", "blk"), None, None)
    return jax.shard_map(
        functools.partial(on_device, mesh.shape["blk"]),
        mesh=mesh,
        in_specs=(flat, P("group"), P("group"), P("group", None)) + (deep,) * 5,
        out_specs=(deep,) * 4 + (flat,),
        check_vma=False,
    )
```

```python
import functools

import jax
import jax.numpy as jnp
from jax import lax
from jax.experimental import pallas as pl
from jax.experimental.pallas import tpu as pltpu
from jax.sharding import PartitionSpec as P

ITERS = 6
SUB = 4
BLK_DEV = 4
BT_DEV = 14
TILES_DEV = 16
LEVELS = 20
ROWS = 32
COLS = 128
TY = 8
STRIP = 16
PACK = 24
TALL = 48
FLOW_VMEM = 47 * 2**20

damping = 0.1
coriolis = 0.3
lowest = 0.02
highest = 2.0

STEPS = [1.0 + 0.1 * k for k in range(LEVELS)]
TOTAL = sum(STEPS)
MESH = pl.DeviceIdType.MESH


def chebyshev_plan(count):
    centre = 0.5 * (highest + lowest)
    spread = 0.5 * (highest - lowest)
    sigma = centre / spread
    rho = 1.0 / sigma
    plan = []
    for _ in range(count):
        fresh = 1.0 / (2.0 * sigma - rho)
        plan.append((fresh * rho, 2.0 * fresh / spread))
        rho = fresh
    return (centre, plan)


def lane_of(shape):
    return lax.broadcasted_iota(jnp.int32, shape, 1)


def row_of(shape):
    return lax.broadcasted_iota(jnp.int32, shape, 0)


def side_pack(field, edge):
    lane = lane_of((TY, COLS))
    out = jnp.zeros((TY, COLS), jnp.float32)
    for group in range(SUB):
        rows = field[group * TY : (group + 1) * TY]
        moved = pltpu.roll(rows, (16 + 32 * group) % COLS, 1)
        out = jnp.where(lane // 32 == group, moved, out)
        if edge is not None:
            moved = pltpu.roll(edge[group * TY : (group + 1) * TY], (1 + 32 * group) % COLS, 1)
            out = jnp.where(lane == 32 * group, moved, out)
    return out


def greet(n, me):
    barrier = pltpu.get_barrier_semaphore()

    def one(k, carry):
        pl.semaphore_signal(
            barrier, inc=1, device_id={"blk": lax.rem(me + k, n)}, device_id_type=MESH
        )
        return carry

    lax.fori_loop(1, n, one, 0)
    pl.semaphore_wait(barrier, n - 1)


class Relay:
    def __init__(self, n, me, x_ref, out_ref, send_sem, recv_sem):
        self.me, self.x, self.out = me, x_ref, out_ref
        self.send_sem, self.recv_sem = send_sem, recv_sem
        self.sent = []
        depth = n // 4
        z, y, c = me // 4, (me // 2) % 2, me % 2

        def at(z, y, c):
            return (z * 2 + y) * 2 + c

        hops = sorted(range(1, depth), key=lambda k: min(k, depth - k))
        far = [lax.rem(z + k, depth) for k in hops]
        self.line = [at(f, y, c) for f in far]
        self.y_peer = at(z, 1 - y, c)
        self.sibling = at(z, y, 1 - c)
        self.cross = [self.y_peer] + [at(f, 1 - y, c) for f in far]
        self.rest = [self.sibling] + [at(f, y, 1 - c) for f in far]
        self.rest += [at(f, 1 - y, 1 - c) for f in [z] + far]
        self.peers = self.line + [self.y_peer, self.sibling]

    def copy(self, source, device, slot, first):
        return pltpu.make_async_remote_copy(
            src_ref=self.x if first else self.out.at[source],
            dst_ref=self.out.at[source],
            send_sem=self.send_sem.at[slot],
            recv_sem=self.recv_sem.at[source],
            device_id={"blk": device},
            device_id_type=MESH,
        )

    def send(self, source, device, first=False):
        copy = self.copy(source, device, len(self.sent), first)
        copy.start()
        self.sent.append(copy)

    def arrived(self, source):
        self.copy(source, self.sibling, 0, False).wait_recv()

    def start(self):
        for peer in self.peers:
            self.send(self.me, peer, True)
        self.out[self.me] = self.x[...]

    def second(self):
        for source in self.line:
            self.arrived(source)
            self.send(source, self.y_peer)
            self.send(source, self.sibling)

    def third(self):
        for source in self.cross:
            self.arrived(source)
            self.send(source, self.sibling)

    def finish(self):
        for source in self.rest:
            self.arrived(source)
        for copy in self.sent:
            copy.wait_send()


def flow_kernel(
    n, wet_hbm, u_hbm, v_hbm, k_hbm, t_hbm, s_hbm,
    um_ref, vm_ref, tm_ref, sm_ref, div_ref, depth_ref, got_div, got_depth,
    wet_ref, u_ref, v_ref, k_ref, t_ref, s_ref,
    ratio_ref, zonal_ref, north_ref, div_pack, depth_pack,
    wet_sem, u_sem, v_sem, k_sem, t_sem, s_sem, div_send, div_recv, depth_send, depth_recv,
):
    me = lax.axis_index("blk")
    relay_depth = Relay(n, me, depth_pack, got_depth, depth_send, depth_recv)
    relay_div = Relay(n, me, div_pack, got_div, div_send, div_recv)
    barrier = pltpu.get_barrier_semaphore()
    for peer in relay_depth.peers:
        pl.semaphore_signal(barrier, inc=1, device_id={"blk": peer}, device_id_type=MESH)
    wet_copy = pltpu.make_async_copy(wet_hbm, wet_ref, wet_sem)
    wet_copy.start()

    flows = ((k_hbm, k_ref, k_sem), (u_hbm, u_ref, u_sem), (v_hbm, v_ref, v_sem))
    tracers = ((t_hbm, t_ref, t_sem), (s_hbm, s_ref, s_sem))

    def fetch(what, block):
        return [
            pltpu.make_async_copy(hbm.at[block], ref.at[block], sem.at[block])
            for hbm, ref, sem in what
        ]

    for what in (flows, tracers):
        for block in range(BLK_DEV):
            for copy in fetch(what, block):
                copy.start()
    wet_copy.wait()
    for block in range(BLK_DEV):
        count = wet_ref[block].astype(jnp.float32)
        depth = (count + 0.05 * (count * (count - 1.0))) * (1.0 / TOTAL)
        depth_ref[block] = depth
        depth_pack[block, 0:8] = depth[0:8]
        depth_pack[block, 8:16] = depth[24:32]
        depth_pack[block, 16:24] = side_pack(depth, None)
    pl.semaphore_wait(barrier, len(relay_depth.peers))
    relay_depth.start()

    def one_block(block, carry):
        for copy in fetch(flows, block):
            copy.wait()

        def strip(index, inner):
            rows = pl.ds(pl.multiple_of(index * STRIP, STRIP), STRIP)
            wet = wet_ref[block, rows, :]
            zero = jnp.zeros((STRIP, COLS), jnp.float32)
            lower = ratio = uv = vv = zero
            for k in range(LEVELS):
                step = STEPS[k]
                u = u_ref[block, k, rows, :]
                v = v_ref[block, k, rows, :]
                if k + 1 < LEVELS:
                    upper = jnp.where(wet > k + 1, k_ref[block, k, rows, :], 0.0)
                else:
                    upper = zero
                inv = 1.0 / (step + upper + lower * (1.0 - ratio))
                scaled = jnp.where(wet > k, step, 0.0)
                uv = (scaled * (u + coriolis * v) + lower * uv) * inv
                vv = (scaled * (v - coriolis * u) + lower * vv) * inv
                ratio = upper * inv
                um_ref[block, k, rows, :] = uv
                vm_ref[block, k, rows, :] = vv
                ratio_ref[k] = ratio
                lower = upper
            last = LEVELS - 1
            zonal = STEPS[last] * uv
            north = STEPS[last] * vv
            for k in range(last - 1, -1, -1):
                ratio = ratio_ref[k]
                uv = um_ref[block, k, rows, :] + ratio * uv
                vv = vm_ref[block, k, rows, :] + ratio * vv
                zonal = zonal + STEPS[k] * uv
                north = north + STEPS[k] * vv
                um_ref[block, k, rows, :] = uv
                vm_ref[block, k, rows, :] = vv
            zonal_ref[rows, :] = zonal * (1.0 / TOTAL)
            north_ref[rows, :] = north * (1.0 / TOTAL)
            return inner

        lax.fori_loop(0, ROWS // STRIP, strip, 0)
        zonal = zonal_ref[...]
        north = north_ref[...]
        lane = lane_of((ROWS, COLS))
        row = row_of((ROWS, COLS))
        left = jnp.where(lane == 0, 0.0, pltpu.roll(zonal, 1, 1))
        above = jnp.where(row == 0, 0.0, pltpu.roll(north, 1, 0))
        div = zonal - left + north - above
        div_ref[block] = div
        div_pack[block, 0:8] = div[0:8]
        div_pack[block, 8:16] = jnp.where(
            row_of((TY, COLS)) == 0, pltpu.roll(north[24:32], 1, 0), div[24:32]
        )
        div_pack[block, 16:24] = side_pack(div, zonal)
        return carry

    def one_tracer(block, carry):
        for copy in fetch(tracers, block):
            copy.wait()

        def strip(index, inner):
            rows = pl.ds(pl.multiple_of(index * STRIP, STRIP), STRIP)
            wet = wet_ref[block, rows, :]
            zero = jnp.zeros((STRIP, COLS), jnp.float32)
            lower = ratio = tv = sv = zero
            for k in range(LEVELS):
                step = STEPS[k]
                if k + 1 < LEVELS:
                    upper = jnp.where(wet > k + 1, 0.5 * k_ref[block, k, rows, :], 0.0)
                else:
                    upper = zero
                inv = 1.0 / (step + upper + lower * (1.0 - ratio))
                tv = (step * t_ref[block, k, rows, :] + lower * tv) * inv
                sv = (step * s_ref[block, k, rows, :] + lower * sv) * inv
                ratio = upper * inv
                tm_ref[block, k, rows, :] = tv
                sm_ref[block, k, rows, :] = sv
                ratio_ref[k] = ratio
                lower = upper
            for k in range(LEVELS - 2, -1, -1):
                ratio = ratio_ref[k]
                tv = tm_ref[block, k, rows, :] + ratio * tv
                sv = sm_ref[block, k, rows, :] + ratio * sv
                tm_ref[block, k, rows, :] = tv
                sm_ref[block, k, rows, :] = sv
            return inner

        lax.fori_loop(0, ROWS // STRIP, strip, 0)
        return carry

    lax.fori_loop(0, 3, one_block, 0)
    relay_depth.second()
    lax.fori_loop(3, BLK_DEV, one_block, 0)
    relay_div.start()
    relay_depth.third()
    lax.fori_loop(0, BLK_DEV, one_tracer, 0)
    relay_div.second()
    relay_div.third()
    relay_depth.finish()
    relay_div.finish()


def flow(n, wet, u, v, kappa, t, s):
    blocks = u.shape[0]
    deep = jax.ShapeDtypeStruct(u.shape, jnp.float32)
    flat = jax.ShapeDtypeStruct((blocks, ROWS, COLS), jnp.float32)
    got = jax.ShapeDtypeStruct((n, blocks, PACK, COLS), jnp.float32)
    vmem = pl.BlockSpec(memory_space=pltpu.VMEM)
    hbm = pl.BlockSpec(memory_space=pltpu.MemorySpace.HBM)
    pack = pltpu.VMEM((blocks, PACK, COLS), jnp.float32)
    return pl.pallas_call(
        functools.partial(flow_kernel, n),
        in_specs=[hbm] * 6,
        out_specs=[vmem] * 8,
        out_shape=[deep, deep, deep, deep, flat, flat, got, got],
        scratch_shapes=[pltpu.VMEM(wet.shape, jnp.int32)]
        + [pltpu.VMEM(u.shape, jnp.float32)] * 5
        + [
            pltpu.VMEM((LEVELS, STRIP, COLS), jnp.float32),
            pltpu.VMEM((ROWS, COLS), jnp.float32),
            pltpu.VMEM((ROWS, COLS), jnp.float32),
            pack,
            pack,
            pltpu.SemaphoreType.DMA,
        ]
        + [pltpu.SemaphoreType.DMA((blocks,))] * 5
        + [pltpu.SemaphoreType.DMA((n,))] * 4,
        compiler_params=pltpu.CompilerParams(
            collective_id=0, has_side_effects=True, vmem_limit_bytes=FLOW_VMEM
        ),
        name="flow",
    )(wet, u, v, kappa, t, s)


def spread_kernel(n, cap, place_ref, x_ref, out_ref, held, send_sem, recv_sem):
    me = lax.axis_index("blk")
    greet(n, me)

    def copy(k):
        other = lax.rem(me + k, n)
        return pltpu.make_async_remote_copy(
            src_ref=x_ref.at[other],
            dst_ref=held.at[me],
            send_sem=send_sem.at[k],
            recv_sem=recv_sem.at[k],
            device_id={"blk": other},
            device_id_type=MESH,
        )

    def begin(k, carry):
        copy(k).start()
        return carry

    def end(k, carry):
        copy(k).wait()
        return carry

    lax.fori_loop(1, n, begin, 0)
    held[me] = x_ref[me]
    lax.fori_loop(1, n, end, 0)
    for slot in range(BT_DEV):
        out_ref[slot] = held[place_ref[2 * slot], place_ref[2 * slot + 1]]


def spread_tiles(n, cap, place, tiles):
    return pl.pallas_call(
        functools.partial(spread_kernel, n, cap),
        out_shape=jax.ShapeDtypeStruct((BT_DEV, TY, COLS), jnp.float32),
        in_specs=[
            pl.BlockSpec(memory_space=pltpu.SMEM),
            pl.BlockSpec(memory_space=pltpu.VMEM),
        ],
        out_specs=pl.BlockSpec(memory_space=pltpu.VMEM),
        scratch_shapes=[
            pltpu.VMEM((n, cap, TY, COLS), jnp.float32),
            pltpu.SemaphoreType.DMA((n,)),
            pltpu.SemaphoreType.DMA((n,)),
        ],
        compiler_params=pltpu.CompilerParams(
            collective_id=1, has_side_effects=True, vmem_limit_bytes=32 * 2**20
        ),
        name="spread_tiles",
    )(place, tiles)


def sideways(main, side, amount):
    lane = lane_of(main.shape)
    edge = lane == (0 if amount == 1 else COLS - 1)
    rolled_main = pltpu.roll(main, amount % COLS, 1)
    rolled_side = pltpu.roll(side, amount % COLS, 1)
    return (
        jnp.where(edge, rolled_side, rolled_main),
        jnp.where(edge, rolled_main, rolled_side),
    )


def ring_sum(main, side):
    rows = main.shape[0]

    def vertical(field):
        return field + 0.25 * (pltpu.roll(field, 1, 0) + pltpu.roll(field, rows - 1, 0))

    vm = vertical(main)
    vs = vertical(side)
    lm, ls = sideways(vm, vs, 1)
    rm, rs = sideways(vm, vs, -1)
    return (
        4.0 * (vm - main) + (lm + rm),
        4.0 * (vs - side) + (ls + rs),
    )


def solve_kernel(
    n, cap, runs_ref, owner_ref, near, got_div, got_depth, div_ref, depth_ref, wet_ref,
    um_ref, vm_ref, tm_ref, sm_ref,
    un_ref, vn_ref, tn_ref, sn_ref, out_ref, place_ref,
    scalars, counts,
):
    step = pl.program_id(0)
    me = lax.axis_index("blk")

    @pl.when(step == 0)
    def _():
        def find(j, found):
            return jnp.where(runs_ref[j * BLK_DEV] == me, j, found)

        run = lax.fori_loop(0, n, find, 0)
        scalars[0] = run
        def clear(j, carry):
            counts[j] = 0
            return carry

        lax.fori_loop(0, n, clear, 0)

        def scan(j, place):
            source = runs_ref[j * BLK_DEV]
            rank = 0
            for a in range(TILES_DEV):
                hit = (owner_ref[j * TILES_DEV + a] == me).astype(jnp.int32)
                place_ref[2 * place] = source
                place_ref[2 * place + 1] = rank
                place = place + hit
                rank = jnp.minimum(rank + hit, cap - 1)
            return place

        lax.fori_loop(0, n, scan, 0)

    run = scalars[0]
    base = step * SUB

    def where_is(tile):
        block = tile // SUB
        there = block < n * BLK_DEV
        safe = jnp.where(there, block, 0)
        return (runs_ref[safe], safe % BLK_DEV, there.astype(jnp.float32))

    first = run * TILES_DEV + base
    final = first + SUB - 1
    above = where_is(near[0, first])
    below = where_is(near[1, final])
    above_left = where_is(near[4, first])
    above_right = where_is(near[5, first])
    below_left = where_is(near[6, final])
    below_right = where_is(near[7, final])
    left_tile = near[2, first]
    right_tile = near[3, first]
    for a in range(1, SUB):
        left_tile = jnp.minimum(left_tile, near[2, first + a])
        right_tile = jnp.minimum(right_tile, near[3, first + a])
    left = where_is(left_tile)
    right = where_is(right_tile)
    own = (me, step, jnp.float32(1.0))

    def load(got, who, start):
        device, slot, there = who
        return got[device, slot, start : start + TY, :] * there

    lane8 = lane_of((TY, COLS))
    row8 = row_of((TY, COLS))

    def corner(got, who_left, who_right, start):
        mixed = jnp.where(lane8 < TY, load(got, who_right, start), load(got, who_left, start))
        return jnp.where((lane8 < TY) | (lane8 >= COLS - TY), mixed, 0.0)

    def beside(got):
        packed = jnp.where(lane8 % 32 >= 16, load(got, right, 16), load(got, left, 16))
        parts = []
        for group in range(SUB):
            moved = pltpu.roll(packed, (112 - 32 * group) % COLS, 1)
            parts.append(jnp.where((lane8 < TY) | (lane8 >= COLS - TY), moved, 0.0))
        return parts

    def edge_column(upper, middle, lower):
        packed = load(got_div, middle, 16)
        parts = [pltpu.roll(load(got_div, upper, 16), 32, 1)]
        for group in range(SUB):
            moved = packed if group == 0 else pltpu.roll(packed, COLS - 32 * group, 1)
            parts.append(moved)
        parts.append(load(got_div, lower, 16))
        return jnp.where(lane48 == 0, jnp.concatenate(parts, axis=0), 0.0)

    lane48 = lane_of((TALL, COLS))
    depth_main = jnp.concatenate(
        [load(got_depth, above, 8), depth_ref[...], load(got_depth, below, 0)], axis=0
    )
    depth_side = jnp.concatenate(
        [corner(got_depth, above_left, above_right, 8)]
        + beside(got_depth)
        + [corner(got_depth, below_left, below_right, 0)],
        axis=0,
    )
    top_main = load(got_div, above, 8)
    top_side = corner(got_div, above_left, above_right, 8)
    first_row = row8 == 0
    mid_main = div_ref[...]
    mid_side = beside(got_div)
    own_main = mid_main[0:8] - jnp.where(first_row, top_main, 0.0)
    mid_side[0] = mid_side[0] - jnp.where(first_row, top_side, 0.0)
    low_main = load(got_div, below, 0) - jnp.where(first_row, load(got_div, own, 8), 0.0)
    low_side = corner(got_div, below_left, below_right, 0) - jnp.where(
        first_row, corner(got_div, left, right, 8), 0.0
    )
    div_main = jnp.concatenate([top_main, own_main, mid_main[8:], low_main], axis=0)
    div_side = jnp.concatenate([top_side] + mid_side + [low_side], axis=0)
    div_main = div_main - edge_column(above_left, left, below_left)
    div_side = div_side - edge_column(above, own, below)

    centre, plan = chebyshev_plan(ITERS)
    depths = (depth_main, depth_side)
    divs = (div_main, div_side)
    ocean = [(d > 0).astype(jnp.float32) for d in depths]
    near_ocean = ring_sum(*ocean)
    near_depth = ring_sum(*depths)
    half = [0.5 * o for o in ocean]
    diagonal = [
        damping + h * (d * a + b) for h, d, a, b in zip(half, depths, near_ocean, near_depth)
    ]
    inverse = [1.0 / x for x in diagonal]
    resid = [-(x * o) for x, o in zip(divs, ocean)]
    search = [r * i * (1.0 / centre) for r, i in zip(resid, inverse)]
    height = [search[0], search[1]]
    for it in range(ITERS - 1):
        around = ring_sum(*search)
        weighted = ring_sum(*[d * s for d, s in zip(depths, search)])
        resid = [
            r - (g * s - h * (d * a + b))
            for r, g, s, h, d, a, b in zip(
                resid, diagonal, search, half, depths, around, weighted
            )
        ]
        first, second = plan[it]
        search = [first * s + second * r * i for s, r, i in zip(search, resid, inverse)]
        height = [e + s for e, s in zip(height, search)]
    eta = height[0][TY : TY + ROWS]
    ocean_mid = ocean[0][TY : TY + ROWS]
    eta_east = sideways(height[0], height[1], -1)[0][TY : TY + ROWS]
    ocean_east = sideways(ocean[0], ocean[1], -1)[0][TY : TY + ROWS]
    eta_south = pltpu.roll(height[0], TALL - 1, 0)[TY : TY + ROWS]
    ocean_south = pltpu.roll(ocean[0], TALL - 1, 0)[TY : TY + ROWS]
    east = (eta_east - eta) * ocean_mid * ocean_east
    south = (eta_south - eta) * ocean_mid * ocean_south

    for a in range(SUB):
        target = owner_ref[run * TILES_DEV + base + a]

        @pl.when(target >= 0)
        def _():
            rank = counts[target]
            counts[target] = rank + 1
            out_ref[target, rank] = eta[a * TY : (a + 1) * TY]

    wet = wet_ref[...]
    for k in range(LEVELS):
        wetted = wet > k
        un_ref[k] = jnp.where(wetted, um_ref[step, k] - east, 0.0)
        vn_ref[k] = jnp.where(wetted, vm_ref[step, k] - south, 0.0)
        tn_ref[k] = jnp.where(wetted, tm_ref[step, k], 0.0)
        sn_ref[k] = jnp.where(wetted, sm_ref[step, k], 0.0)


def solve(n, cap, patch_owner, piece_owner, near, got_div, got_depth, div, depth, wet, fields):
    blocks = wet.shape[0]
    deep = pl.BlockSpec((None, LEVELS, ROWS, COLS), lambda i: (i, 0, 0, 0))
    flat = pl.BlockSpec((None, ROWS, COLS), lambda i: (i, 0, 0))
    deep_shape = jax.ShapeDtypeStruct(fields[0].shape, jnp.float32)
    smem = pl.BlockSpec(memory_space=pltpu.SMEM)
    vmem = pl.BlockSpec(memory_space=pltpu.VMEM)
    return pl.pallas_call(
        functools.partial(solve_kernel, n, cap),
        grid=(blocks,),
        in_specs=[smem] * 3 + [vmem] * 2 + [flat] * 3 + [vmem] * 4,
        out_specs=[deep] * 4 + [pl.BlockSpec((n, cap, TY, COLS), lambda i: (0, 0, 0, 0)), smem],
        out_shape=[deep_shape] * 4
        + [
            jax.ShapeDtypeStruct((n, cap, TY, COLS), jnp.float32),
            jax.ShapeDtypeStruct((2 * BT_DEV + 4,), jnp.int32),
        ],
        scratch_shapes=[pltpu.SMEM((1,), jnp.int32), pltpu.SMEM((n,), jnp.int32)],
        compiler_params=pltpu.CompilerParams(vmem_limit_bytes=40 * 2**20),
        name="solve",
    )(patch_owner, piece_owner, near, got_div, got_depth, div, depth, wet, *fields)


def on_device(n, wet, patch_owner, piece_owner, neighbours, u, v, t, s, kappa):
    cap = max(2, TILES_DEV // n)
    um, vm, tm, sm, div, depth, got_div, got_depth = flow(n, wet, u, v, kappa, t, s)
    un, vn, tn, sn, tiles, place = solve(
        n, cap, patch_owner, piece_owner, neighbours.T,
        got_div, got_depth, div, depth, wet, (um, vm, tm, sm),
    )
    height = spread_tiles(n, cap, place, tiles)
    return (un, vn, tn, sn, height)


def solution(mesh):
    deep = P(("group", "blk"), None, None, None)
    flat = P(("group", "blk"), None, None)
    return jax.shard_map(
        functools.partial(on_device, mesh.shape["blk"]),
        mesh=mesh,
        in_specs=(flat, P("group"), P("group"), P("group", None)) + (deep,) * 5,
        out_specs=(deep,) * 4 + (flat,),
        check_vma=False,
    )
```

```python
import functools

import jax
import jax.numpy as jnp
from jax import lax
from jax.experimental import pallas as pl
from jax.experimental.pallas import tpu as pltpu
from jax.sharding import PartitionSpec as P

ITERS = 6
SUB = 4
BLK_DEV = 4
BT_DEV = 14
TILES_DEV = 16
LEVELS = 20
ROWS = 32
COLS = 128
TY = 8
STRIP = 16
PACK = 24
TALL = 48
FLOW_VMEM = 95 * 2**19

damping = 0.1
coriolis = 0.3
lowest = 0.02
highest = 2.0

STEPS = [1.0 + 0.1 * k for k in range(LEVELS)]
TOTAL = sum(STEPS)
MESH = pl.DeviceIdType.MESH


def chebyshev_plan(count):
    centre = 0.5 * (highest + lowest)
    spread = 0.5 * (highest - lowest)
    sigma = centre / spread
    rho = 1.0 / sigma
    plan = []
    for _ in range(count):
        fresh = 1.0 / (2.0 * sigma - rho)
        plan.append((fresh * rho, 2.0 * fresh / spread))
        rho = fresh
    return (centre, plan)


def lane_of(shape):
    return lax.broadcasted_iota(jnp.int32, shape, 1)


def row_of(shape):
    return lax.broadcasted_iota(jnp.int32, shape, 0)


def side_pack(div, depth, edge):
    lane = lane_of((TY, COLS))
    out = jnp.zeros((TY, COLS), jnp.float32)
    for group in range(SUB):
        rows = slice(group * TY, (group + 1) * TY)
        moved = pltpu.roll(div[rows], 8 + 32 * group, 1)
        out = jnp.where(lane // 16 == 2 * group, moved, out)
        moved = pltpu.roll(depth[rows], (24 + 32 * group) % COLS, 1)
        out = jnp.where(lane // 16 == 2 * group + 1, moved, out)
        moved = pltpu.roll(edge[rows], 1 + 32 * group, 1)
        out = jnp.where(lane == 32 * group, moved, out)
    return out


def greet(n, me):
    barrier = pltpu.get_barrier_semaphore()

    def one(k, carry):
        pl.semaphore_signal(
            barrier, inc=1, device_id={"blk": lax.rem(me + k, n)}, device_id_type=MESH
        )
        return carry

    lax.fori_loop(1, n, one, 0)
    pl.semaphore_wait(barrier, n - 1)


class Relay:
    def __init__(self, n, me, x_ref, out_ref, send_sem, recv_sem):
        self.me, self.x, self.out = me, x_ref, out_ref
        self.send_sem, self.recv_sem = send_sem, recv_sem
        self.sent = []
        depth = n // 4
        z, y, c = me // 4, (me // 2) % 2, me % 2

        def at(z, y, c):
            return (z * 2 + y) * 2 + c

        hops = sorted(range(1, depth), key=lambda k: min(k, depth - k))
        far = [lax.rem(z + k, depth) for k in hops]
        self.line = [at(f, y, c) for f in far]
        self.y_peer = at(z, 1 - y, c)
        self.sibling = at(z, y, 1 - c)
        self.cross = [self.y_peer] + [at(f, 1 - y, c) for f in far]
        self.rest = [self.sibling] + [at(f, y, 1 - c) for f in far]
        self.rest += [at(f, 1 - y, 1 - c) for f in [z] + far]
        self.peers = self.line + [self.y_peer, self.sibling]

    def copy(self, source, device, slot, first):
        return pltpu.make_async_remote_copy(
            src_ref=self.x if first else self.out.at[source],
            dst_ref=self.out.at[source],
            send_sem=self.send_sem.at[slot],
            recv_sem=self.recv_sem.at[source],
            device_id={"blk": device},
            device_id_type=MESH,
        )

    def send(self, source, device, first=False):
        copy = self.copy(source, device, len(self.sent), first)
        copy.start()
        self.sent.append(copy)

    def arrived(self, source):
        self.copy(source, self.sibling, 0, False).wait_recv()

    def start(self):
        for peer in self.peers:
            self.send(self.me, peer, True)
        self.out[self.me] = self.x[...]

    def second(self):
        for source in self.line:
            self.arrived(source)
            self.send(source, self.y_peer)
            self.send(source, self.sibling)

    def third(self):
        for source in self.cross:
            self.arrived(source)
            self.send(source, self.sibling)

    def finish(self):
        for source in self.rest:
            self.arrived(source)
        for copy in self.sent:
            copy.wait_send()


def flow_kernel(
    n, wet_hbm, u_hbm, v_hbm, k_hbm, t_hbm, s_hbm,
    um_ref, vm_ref, tm_ref, sm_ref, div_ref, depth_ref, got_div, got_depth,
    wet_ref, u_ref, v_ref, k_ref, t_ref, s_ref,
    ratio_ref, zonal_ref, north_ref, div_pack, depth_pack,
    wet_sem, u_sem, v_sem, k_sem, t_sem, s_sem, div_send, div_recv, depth_send, depth_recv,
):
    me = lax.axis_index("blk")
    relay_depth = Relay(n, me, depth_pack, got_depth, depth_send, depth_recv)
    relay_div = Relay(n, me, div_pack, got_div, div_send, div_recv)
    barrier = pltpu.get_barrier_semaphore()
    for peer in relay_depth.peers:
        pl.semaphore_signal(barrier, inc=1, device_id={"blk": peer}, device_id_type=MESH)
    wet_copy = pltpu.make_async_copy(wet_hbm, wet_ref, wet_sem)
    wet_copy.start()

    flows = ((k_hbm, k_ref, k_sem), (u_hbm, u_ref, u_sem), (v_hbm, v_ref, v_sem))
    tracers = ((t_hbm, t_ref, t_sem), (s_hbm, s_ref, s_sem))

    def fetch(what, block):
        return [
            pltpu.make_async_copy(hbm.at[block], ref.at[block], sem.at[block])
            for hbm, ref, sem in what
        ]

    for what in (flows, tracers):
        for block in range(BLK_DEV):
            for copy in fetch(what, block):
                copy.start()
    wet_copy.wait()
    for block in range(BLK_DEV):
        count = wet_ref[block].astype(jnp.float32)
        depth = (count + 0.05 * (count * (count - 1.0))) * (1.0 / TOTAL)
        depth_ref[block] = depth
        depth_pack[block, 0:8] = depth[0:8]
        depth_pack[block, 8:16] = depth[24:32]
    pl.semaphore_wait(barrier, len(relay_depth.peers))
    relay_depth.start()

    def one_block(block, carry):
        for copy in fetch(flows, block):
            copy.wait()

        def strip(index, inner):
            rows = pl.ds(pl.multiple_of(index * STRIP, STRIP), STRIP)
            wet = wet_ref[block, rows, :]
            zero = jnp.zeros((STRIP, COLS), jnp.float32)
            lower = ratio = uv = vv = zero
            for k in range(LEVELS):
                step = STEPS[k]
                u = u_ref[block, k, rows, :]
                v = v_ref[block, k, rows, :]
                if k + 1 < LEVELS:
                    upper = jnp.where(wet > k + 1, k_ref[block, k, rows, :], 0.0)
                else:
                    upper = zero
                inv = 1.0 / (step + upper + lower * (1.0 - ratio))
                scaled = jnp.where(wet > k, step, 0.0)
                uv = (scaled * (u + coriolis * v) + lower * uv) * inv
                vv = (scaled * (v - coriolis * u) + lower * vv) * inv
                ratio = upper * inv
                um_ref[block, k, rows, :] = uv
                vm_ref[block, k, rows, :] = vv
                ratio_ref[k] = ratio
                lower = upper
            last = LEVELS - 1
            zonal = STEPS[last] * uv
            north = STEPS[last] * vv
            for k in range(last - 1, -1, -1):
                ratio = ratio_ref[k]
                uv = um_ref[block, k, rows, :] + ratio * uv
                vv = vm_ref[block, k, rows, :] + ratio * vv
                zonal = zonal + STEPS[k] * uv
                north = north + STEPS[k] * vv
                um_ref[block, k, rows, :] = uv
                vm_ref[block, k, rows, :] = vv
            zonal_ref[rows, :] = zonal * (1.0 / TOTAL)
            north_ref[rows, :] = north * (1.0 / TOTAL)
            return inner

        lax.fori_loop(0, ROWS // STRIP, strip, 0)
        zonal = zonal_ref[...]
        north = north_ref[...]
        lane = lane_of((ROWS, COLS))
        row = row_of((ROWS, COLS))
        left = jnp.where(lane == 0, 0.0, pltpu.roll(zonal, 1, 1))
        above = jnp.where(row == 0, 0.0, pltpu.roll(north, 1, 0))
        div = zonal - left + north - above
        div_ref[block] = div
        div_pack[block, 0:8] = div[0:8]
        div_pack[block, 8:16] = jnp.where(
            row_of((TY, COLS)) == 0, pltpu.roll(north[24:32], 1, 0), div[24:32]
        )
        div_pack[block, 16:24] = side_pack(div, depth_ref[block], zonal)
        return carry

    def one_tracer(block, carry):
        for copy in fetch(tracers, block):
            copy.wait()

        def strip(index, inner):
            rows = pl.ds(pl.multiple_of(index * STRIP, STRIP), STRIP)
            wet = wet_ref[block, rows, :]
            zero = jnp.zeros((STRIP, COLS), jnp.float32)
            lower = ratio = tv = sv = zero
            for k in range(LEVELS):
                step = STEPS[k]
                if k + 1 < LEVELS:
                    upper = jnp.where(wet > k + 1, 0.5 * k_ref[block, k, rows, :], 0.0)
                else:
                    upper = zero
                inv = 1.0 / (step + upper + lower * (1.0 - ratio))
                tv = (step * t_ref[block, k, rows, :] + lower * tv) * inv
                sv = (step * s_ref[block, k, rows, :] + lower * sv) * inv
                ratio = upper * inv
                tm_ref[block, k, rows, :] = tv
                sm_ref[block, k, rows, :] = sv
                ratio_ref[k] = ratio
                lower = upper
            for k in range(LEVELS - 2, -1, -1):
                ratio = ratio_ref[k]
                tv = tm_ref[block, k, rows, :] + ratio * tv
                sv = sm_ref[block, k, rows, :] + ratio * sv
                tm_ref[block, k, rows, :] = tv
                sm_ref[block, k, rows, :] = sv
            return inner

        lax.fori_loop(0, ROWS // STRIP, strip, 0)
        return carry

    lax.fori_loop(0, BLK_DEV, one_block, 0)
    relay_div.start()
    relay_depth.second()
    lax.fori_loop(0, BLK_DEV, one_tracer, 0)
    relay_div.second()
    relay_depth.third()
    relay_div.third()
    relay_depth.finish()
    relay_div.finish()


def flow(n, wet, u, v, kappa, t, s):
    blocks = u.shape[0]
    deep = jax.ShapeDtypeStruct(u.shape, jnp.float32)
    flat = jax.ShapeDtypeStruct((blocks, ROWS, COLS), jnp.float32)
    got_div = jax.ShapeDtypeStruct((n, blocks, PACK, COLS), jnp.float32)
    got_depth = jax.ShapeDtypeStruct((n, blocks, 2 * TY, COLS), jnp.float32)
    vmem = pl.BlockSpec(memory_space=pltpu.VMEM)
    hbm = pl.BlockSpec(memory_space=pltpu.MemorySpace.HBM)
    return pl.pallas_call(
        functools.partial(flow_kernel, n),
        in_specs=[hbm] * 6,
        out_specs=[vmem] * 8,
        out_shape=[deep, deep, deep, deep, flat, flat, got_div, got_depth],
        scratch_shapes=[pltpu.VMEM(wet.shape, jnp.int32)]
        + [pltpu.VMEM(u.shape, jnp.float32)] * 5
        + [
            pltpu.VMEM((LEVELS, STRIP, COLS), jnp.float32),
            pltpu.VMEM((ROWS, COLS), jnp.float32),
            pltpu.VMEM((ROWS, COLS), jnp.float32),
            pltpu.VMEM((blocks, PACK, COLS), jnp.float32),
            pltpu.VMEM((blocks, 2 * TY, COLS), jnp.float32),
            pltpu.SemaphoreType.DMA,
        ]
        + [pltpu.SemaphoreType.DMA((blocks,))] * 5
        + [pltpu.SemaphoreType.DMA((n,))] * 4,
        compiler_params=pltpu.CompilerParams(
            collective_id=0, has_side_effects=True, vmem_limit_bytes=FLOW_VMEM
        ),
        name="flow",
    )(wet, u, v, kappa, t, s)


def spread_kernel(n, cap, place_ref, x_ref, out_ref, held, send_sem, recv_sem):
    me = lax.axis_index("blk")
    greet(n, me)

    def copy(k):
        other = lax.rem(me + k, n)
        return pltpu.make_async_remote_copy(
            src_ref=x_ref.at[other],
            dst_ref=held.at[me],
            send_sem=send_sem.at[k],
            recv_sem=recv_sem.at[k],
            device_id={"blk": other},
            device_id_type=MESH,
        )

    def begin(k, carry):
        copy(k).start()
        return carry

    def end(k, carry):
        copy(k).wait()
        return carry

    lax.fori_loop(1, n, begin, 0)
    held[me] = x_ref[me]
    lax.fori_loop(1, n, end, 0)
    for slot in range(BT_DEV):
        out_ref[slot] = held[place_ref[2 * slot], place_ref[2 * slot + 1]]


def spread_tiles(n, cap, place, tiles):
    return pl.pallas_call(
        functools.partial(spread_kernel, n, cap),
        out_shape=jax.ShapeDtypeStruct((BT_DEV, TY, COLS), jnp.float32),
        in_specs=[
            pl.BlockSpec(memory_space=pltpu.SMEM),
            pl.BlockSpec(memory_space=pltpu.VMEM),
        ],
        out_specs=pl.BlockSpec(memory_space=pltpu.VMEM),
        scratch_shapes=[
            pltpu.VMEM((n, cap, TY, COLS), jnp.float32),
            pltpu.SemaphoreType.DMA((n,)),
            pltpu.SemaphoreType.DMA((n,)),
        ],
        compiler_params=pltpu.CompilerParams(
            collective_id=1, has_side_effects=True, vmem_limit_bytes=32 * 2**20
        ),
        name="spread_tiles",
    )(place, tiles)


def sideways(main, side, amount):
    lane = lane_of(main.shape)
    edge = lane == (0 if amount == 1 else COLS - 1)
    rolled_main = pltpu.roll(main, amount % COLS, 1)
    rolled_side = pltpu.roll(side, amount % COLS, 1)
    return (
        jnp.where(edge, rolled_side, rolled_main),
        jnp.where(edge, rolled_main, rolled_side),
    )


def ring_sum(main, side):
    rows = main.shape[0]

    def vertical(field):
        return field + 0.25 * (pltpu.roll(field, 1, 0) + pltpu.roll(field, rows - 1, 0))

    vm = vertical(main)
    vs = vertical(side)
    lm, ls = sideways(vm, vs, 1)
    rm, rs = sideways(vm, vs, -1)
    return (
        4.0 * (vm - main) + (lm + rm),
        4.0 * (vs - side) + (ls + rs),
    )


def solve_kernel(
    n, cap, runs_ref, owner_ref, near, got_div, got_depth, div_ref, depth_ref, wet_ref,
    um_ref, vm_ref, tm_ref, sm_ref,
    un_ref, vn_ref, tn_ref, sn_ref, out_ref, place_ref,
    scalars, counts,
):
    step = pl.program_id(0)
    me = lax.axis_index("blk")

    @pl.when(step == 0)
    def _():
        def find(j, found):
            return jnp.where(runs_ref[j * BLK_DEV] == me, j, found)

        run = lax.fori_loop(0, n, find, 0)
        scalars[0] = run
        def clear(j, carry):
            counts[j] = 0
            return carry

        lax.fori_loop(0, n, clear, 0)

        scalars[1] = 0

    place = scalars[1]
    share = n // BLK_DEV
    for part in range(share):
        j = step * share + part
        source = runs_ref[j * BLK_DEV]
        rank = 0
        for a in range(TILES_DEV):
            hit = (owner_ref[j * TILES_DEV + a] == me).astype(jnp.int32)
            place_ref[2 * place] = source
            place_ref[2 * place + 1] = rank
            place = place + hit
            rank = jnp.minimum(rank + hit, cap - 1)
    scalars[1] = place
    run = scalars[0]
    base = step * SUB

    def where_is(tile):
        block = tile // SUB
        there = block < n * BLK_DEV
        safe = jnp.where(there, block, 0)
        return (runs_ref[safe], safe % BLK_DEV, there.astype(jnp.float32))

    first = run * TILES_DEV + base
    final = first + SUB - 1
    above = where_is(near[0, first])
    below = where_is(near[1, final])
    above_left = where_is(near[4, first])
    above_right = where_is(near[5, first])
    below_left = where_is(near[6, final])
    below_right = where_is(near[7, final])
    left_tile = near[2, first]
    right_tile = near[3, first]
    for a in range(1, SUB):
        left_tile = jnp.minimum(left_tile, near[2, first + a])
        right_tile = jnp.minimum(right_tile, near[3, first + a])
    left = where_is(left_tile)
    right = where_is(right_tile)
    own = (me, step, jnp.float32(1.0))

    def load(got, who, start):
        device, slot, there = who
        return got[device, slot, start : start + TY, :] * there

    lane8 = lane_of((TY, COLS))
    row8 = row_of((TY, COLS))

    def corner(got, who_left, who_right, start):
        mixed = jnp.where(lane8 < TY, load(got, who_right, start), load(got, who_left, start))
        return jnp.where((lane8 < TY) | (lane8 >= COLS - TY), mixed, 0.0)

    def beside(offset):
        packed = jnp.where(
            lane8 % 32 >= offset, load(got_div, right, 16), load(got_div, left, 16)
        )
        parts = []
        for group in range(SUB):
            moved = pltpu.roll(packed, (COLS - offset - 32 * group) % COLS, 1)
            parts.append(jnp.where((lane8 < TY) | (lane8 >= COLS - TY), moved, 0.0))
        return parts

    def edge_column(upper, middle, lower):
        packed = load(got_div, middle, 16)
        parts = [pltpu.roll(load(got_div, upper, 16), 32, 1)]
        for group in range(SUB):
            moved = packed if group == 0 else pltpu.roll(packed, COLS - 32 * group, 1)
            parts.append(moved)
        parts.append(load(got_div, lower, 16))
        return jnp.where(lane48 == 0, jnp.concatenate(parts, axis=0), 0.0)

    lane48 = lane_of((TALL, COLS))
    depth_main = jnp.concatenate(
        [load(got_depth, above, 8), depth_ref[...], load(got_depth, below, 0)], axis=0
    )
    depth_side = jnp.concatenate(
        [corner(got_depth, above_left, above_right, 8)]
        + beside(24)
        + [corner(got_depth, below_left, below_right, 0)],
        axis=0,
    )
    top_main = load(got_div, above, 8)
    top_side = corner(got_div, above_left, above_right, 8)
    first_row = row8 == 0
    mid_main = div_ref[...]
    mid_side = beside(8)
    own_main = mid_main[0:8] - jnp.where(first_row, top_main, 0.0)
    mid_side[0] = mid_side[0] - jnp.where(first_row, top_side, 0.0)
    low_main = load(got_div, below, 0) - jnp.where(first_row, load(got_div, own, 8), 0.0)
    low_side = corner(got_div, below_left, below_right, 0) - jnp.where(
        first_row, corner(got_div, left, right, 8), 0.0
    )
    div_main = jnp.concatenate([top_main, own_main, mid_main[8:], low_main], axis=0)
    div_side = jnp.concatenate([top_side] + mid_side + [low_side], axis=0)
    div_main = div_main - edge_column(above_left, left, below_left)
    div_side = div_side - edge_column(above, own, below)

    centre, plan = chebyshev_plan(ITERS)
    depths = (depth_main, depth_side)
    divs = (div_main, div_side)
    ocean = [(d > 0).astype(jnp.float32) for d in depths]
    near_ocean = ring_sum(*ocean)
    near_depth = ring_sum(*depths)
    half = [0.5 * o for o in ocean]
    diagonal = [
        damping + h * (d * a + b) for h, d, a, b in zip(half, depths, near_ocean, near_depth)
    ]
    inverse = [1.0 / x for x in diagonal]
    resid = [-(x * o) for x, o in zip(divs, ocean)]
    search = [r * i * (1.0 / centre) for r, i in zip(resid, inverse)]
    height = [search[0], search[1]]
    for it in range(ITERS - 1):
        around = ring_sum(*search)
        weighted = ring_sum(*[d * s for d, s in zip(depths, search)])
        resid = [
            r - (g * s - h * (d * a + b))
            for r, g, s, h, d, a, b in zip(
                resid, diagonal, search, half, depths, around, weighted
            )
        ]
        first, second = plan[it]
        search = [first * s + second * r * i for s, r, i in zip(search, resid, inverse)]
        height = [e + s for e, s in zip(height, search)]
    eta = height[0][TY : TY + ROWS]
    ocean_mid = ocean[0][TY : TY + ROWS]
    eta_east = sideways(height[0], height[1], -1)[0][TY : TY + ROWS]
    ocean_east = sideways(ocean[0], ocean[1], -1)[0][TY : TY + ROWS]
    eta_south = pltpu.roll(height[0], TALL - 1, 0)[TY : TY + ROWS]
    ocean_south = pltpu.roll(ocean[0], TALL - 1, 0)[TY : TY + ROWS]
    east = (eta_east - eta) * ocean_mid * ocean_east
    south = (eta_south - eta) * ocean_mid * ocean_south

    for a in range(SUB):
        target = owner_ref[run * TILES_DEV + base + a]

        @pl.when(target >= 0)
        def _():
            rank = counts[target]
            counts[target] = rank + 1
            out_ref[target, rank] = eta[a * TY : (a + 1) * TY]

    wet = wet_ref[...]
    for k in range(LEVELS):
        wetted = wet > k
        un_ref[k] = jnp.where(wetted, um_ref[step, k] - east, 0.0)
        vn_ref[k] = jnp.where(wetted, vm_ref[step, k] - south, 0.0)
        tn_ref[k] = jnp.where(wetted, tm_ref[step, k], 0.0)
        sn_ref[k] = jnp.where(wetted, sm_ref[step, k], 0.0)


def solve(n, cap, patch_owner, piece_owner, near, got_div, got_depth, div, depth, wet, fields):
    blocks = wet.shape[0]
    deep = pl.BlockSpec((None, LEVELS, ROWS, COLS), lambda i: (i, 0, 0, 0))
    flat = pl.BlockSpec((None, ROWS, COLS), lambda i: (i, 0, 0))
    deep_shape = jax.ShapeDtypeStruct(fields[0].shape, jnp.float32)
    smem = pl.BlockSpec(memory_space=pltpu.SMEM)
    vmem = pl.BlockSpec(memory_space=pltpu.VMEM)
    return pl.pallas_call(
        functools.partial(solve_kernel, n, cap),
        grid=(blocks,),
        in_specs=[smem] * 3 + [vmem] * 2 + [flat] * 3 + [vmem] * 4,
        out_specs=[deep] * 4 + [pl.BlockSpec((n, cap, TY, COLS), lambda i: (0, 0, 0, 0)), smem],
        out_shape=[deep_shape] * 4
        + [
            jax.ShapeDtypeStruct((n, cap, TY, COLS), jnp.float32),
            jax.ShapeDtypeStruct((2 * BT_DEV + 4,), jnp.int32),
        ],
        scratch_shapes=[pltpu.SMEM((2,), jnp.int32), pltpu.SMEM((n,), jnp.int32)],
        compiler_params=pltpu.CompilerParams(vmem_limit_bytes=40 * 2**20),
        name="solve",
    )(patch_owner, piece_owner, near, got_div, got_depth, div, depth, wet, *fields)


def on_device(n, wet, patch_owner, piece_owner, neighbours, u, v, t, s, kappa):
    cap = max(2, TILES_DEV // n)
    um, vm, tm, sm, div, depth, got_div, got_depth = flow(n, wet, u, v, kappa, t, s)
    un, vn, tn, sn, tiles, place = solve(
        n, cap, patch_owner, piece_owner, neighbours.T,
        got_div, got_depth, div, depth, wet, (um, vm, tm, sm),
    )
    height = spread_tiles(n, cap, place, tiles)
    return (un, vn, tn, sn, height)


def solution(mesh):
    deep = P(("group", "blk"), None, None, None)
    flat = P(("group", "blk"), None, None)
    return jax.shard_map(
        functools.partial(on_device, mesh.shape["blk"]),
        mesh=mesh,
        in_specs=(flat, P("group"), P("group"), P("group", None)) + (deep,) * 5,
        out_specs=(deep,) * 4 + (flat,),
        check_vma=False,
    )
```
